128 devices in a mesh: gx: 32 (over y_hi, z, x), gy: 4 (over y_lo, core).
Axes of the slice: x: 4, y: 4 (y_hi: 2, y_lo: 2; y = y_hi * 2 + y_lo), z: 4, core: 2. Of those that a mesh axis runs over, the one named last changes fastest.
Arguments:
- coarse_input: bfloat16 [128, 32, 8, 128], P(None, 'gx', 'gy'), may hold values from -6 to 6
- upsampled: bfloat16 [64, 64, 16, 256], P(None, 'gx', 'gy'), may hold values from -6 to 6
- hidden_one: bfloat16 [64, 64, 16, 256], P(None, 'gx', 'gy'), may hold values from 0 to 6, as said below
- hidden_two: bfloat16 [64, 64, 16, 256], P(None, 'gx', 'gy'), may hold values from 0 to 6, as said below
- cotangent: bfloat16 [64, 64, 16, 256], P(None, 'gx', 'gy'), may hold values from -6 to 6
- tconv_weight: bfloat16 [64, 64, 128], replicated, may hold values from -0.1875 to 0.1875
- conv_one_weight: bfloat16 [27, 64, 64], replicated, may hold values from -0.15625 to 0.15625
- conv_two_weight: bfloat16 [27, 64, 64], replicated, may hold values from -0.15625 to 0.15625
Outputs:
- input_grad: bfloat16 [128, 32, 8, 128], P(None, 'gx', 'gy')
- tconv_grad: float32 [64, 64, 128], replicated
- conv_one_grad: float32 [27, 64, 64], replicated
- conv_two_grad: float32 [27, 64, 64], replicated
The draws below stay inside these ranges and needn't reach their ends.
Inputs may be any that keep to these rules, and one draw needn't show every extreme that they name: `hidden_one`: ReLU-like activations; about half of the entries are zero. `hidden_two`: ReLU-like activations; about half of the entries are zero.
All inputs are finite; a program needn't handle non-finite values.
Results may differ from the reference program's by a relative error of at most 0.0057.
Values may be sent and summed in bfloat16 or wider, within the bound.
A program may use at most 128 MiB of HBM per device.

```python
import math
import jax
import jax.numpy as jnp

C = 64
CIN = 128
NZ = 256
NX = 64
NY = 16


def draw_hidden_one(key, part):
    key = jax.random.fold_in(key, 11)
    values = jax.random.normal(key, (C, NX, NY, NZ), jnp.float32)
    return jnp.clip(values, 0.0, 6.0).astype(jnp.bfloat16)


def draw_hidden_two(key, part):
    key = jax.random.fold_in(key, 23)
    values = jax.random.normal(key, (C, NX, NY, NZ), jnp.float32)
    return jnp.clip(values, 0.0, 6.0).astype(jnp.bfloat16)


def level_of(stream_key, dims, cuts, least, largest):
    loudness, own = 1.0, jax.random.fold_in(stream_key, 6)
    for axis_at, blocks in cuts:
        draws = jnp.exp(jax.random.uniform(jax.random.fold_in(own, axis_at), (blocks,), jnp.float32, least / len(cuts), largest / len(cuts)))
        loudness = loudness * jnp.repeat(draws, dims[axis_at] // blocks).reshape([-1 if axis == axis_at else 1 for axis in range(len(dims))])
    return loudness


def noise(key, shape, scale, limit, cuts=(), held_as=jnp.bfloat16):
    drawn = scale * jax.random.normal(key, shape, jnp.float32)
    if cuts:
        drawn = drawn * level_of(key, shape, cuts, -0.22, 0.18)
    return jnp.clip(drawn, -limit, limit).astype(held_as)


def setup_inputs(seed: int = 0) -> dict:
    key_of = jax.random.split(jax.random.key(seed), 9)
    coarse_input = noise(key_of[0], (CIN, NX // 2, NY // 2, NZ // 2), 1.0, 6.0, ((1, 32), (2, 4)))
    upsampled = noise(key_of[1], (C, NX, NY, NZ), 1.0, 6.0, ((1, 32), (2, 4)))
    hidden_one = draw_hidden_one(jax.random.fold_in(key_of[8], 71), 0)
    hidden_two = draw_hidden_two(jax.random.fold_in(key_of[8], 71), 0)
    cotangent = noise(key_of[4], (C, NX, NY, NZ), 1.0, 6.0, ((1, 32), (2, 4)))
    tconv_weight = noise(key_of[5], (64, C, CIN), (8 * CIN) ** -0.5, 0.1875)
    conv_one_weight = noise(key_of[6], (27, C, C), (27 * C) ** -0.5, 0.15625)
    conv_two_weight = noise(key_of[7], (27, C, C), (27 * C) ** -0.5, 0.15625)
    return {"coarse_input": coarse_input, "upsampled": upsampled, "hidden_one": hidden_one, "hidden_two": hidden_two, "cotangent": cotangent, "tconv_weight": tconv_weight, "conv_one_weight": conv_one_weight, "conv_two_weight": conv_two_weight}


def conv_grads(source, delta, weight, scale):
    planes, across, length = (source.shape[1], source.shape[2], source.shape[3])
    source_pad = jnp.pad(source, ((0, 0), (1, 1), (1, 1), (1, 1)))
    delta_pad = jnp.pad(delta, ((0, 0), (1, 1), (1, 1), (1, 1)))
    delta_wide = delta.astype(jnp.float32)
    weight_grads = []
    backward = jnp.zeros(source.shape, jnp.float32)
    for tap_index in range(27):
        offset_x, offset_y, offset_z = (tap_index // 9, tap_index // 3 % 3, tap_index % 3)
        window = source_pad[:, offset_x:offset_x + planes, offset_y:offset_y + across, offset_z:offset_z + length]
        weight_grads.append(jnp.einsum('opqr,ipqr->oi', delta_wide, window.astype(jnp.float32)))
        shifted = delta_pad[:, 2 - offset_x:2 - offset_x + planes, 2 - offset_y:2 - offset_y + across, 2 - offset_z:2 - offset_z + length]
        backward = backward + jnp.einsum('oi,opqr->ipqr', weight[tap_index].astype(jnp.float32), shifted.astype(jnp.float32))
    return (jnp.stack(weight_grads, 0) * scale, backward)

def reference(coarse_input, upsampled, hidden_one, hidden_two, cotangent, tconv_weight, conv_one_weight, conv_two_weight):
    scale = 1.0 / math.sqrt(NX * NY * NZ)
    delta_two = jnp.where(hidden_two > 0, cotangent, jnp.zeros_like(cotangent))
    conv_two_grad, hidden_grad = conv_grads(hidden_one, delta_two, conv_two_weight, scale)
    delta_one = jnp.where(hidden_one > 0, hidden_grad, jnp.zeros_like(hidden_grad)).astype(jnp.bfloat16)
    conv_one_grad, up_grad = conv_grads(upsampled, delta_one, conv_one_weight, scale)
    upsampled_grad = up_grad.astype(jnp.bfloat16)
    grad_pad = jnp.pad(upsampled_grad, ((0, 0), (1, 1), (1, 1), (1, 1)))
    coarse_wide = coarse_input.astype(jnp.float32)
    tconv_parts = []
    input_sum = jnp.zeros(coarse_input.shape, jnp.float32)
    for tap_index in range(64):
        start_x, start_y, start_z = (tap_index // 16, tap_index // 4 % 4, tap_index % 4)
        piece = grad_pad[:, start_x:start_x + NX:2, start_y:start_y + NY:2, start_z:start_z + NZ:2].astype(jnp.float32)
        tconv_parts.append(jnp.einsum('opqr,ipqr->oi', piece, coarse_wide))
        input_sum = input_sum + jnp.einsum('oi,opqr->ipqr', tconv_weight[tap_index].astype(jnp.float32), piece)
    tconv_grad = jnp.stack(tconv_parts, 0) * scale
    return (input_sum.astype(jnp.bfloat16), tconv_grad, conv_one_grad, conv_two_grad)
```

```python
import functools
import math

import jax
import jax.numpy as jnp
from jax import lax
from jax.experimental import pallas as pl
from jax.experimental.pallas import tpu as pltpu
from jax.sharding import PartitionSpec as P

BF16 = jnp.bfloat16
F32 = jnp.float32
MESH = pl.DeviceIdType.MESH
SIDES = [(dx, dy) for dx in (-1, 0, 1) for dy in (-1, 0, 1) if dx or dy]
VMEM_BYTES = 56 * 1024 * 1024

TCONV_ROWS = 4096
CONV_ROWS = 576
ROWS = 6144
HALF = ROWS // 2
PART = HALF // 3


def nn(a, b):
    return lax.dot_general(a, b, (((1,), (0,)), ((), ())), preferred_element_type=F32)


def nt(a, b):
    return lax.dot_general(a, b, (((1,), (1,)), ((), ())), preferred_element_type=F32)


def moved(cells, by):
    length = cells.shape[-1]
    lane = lax.broadcasted_iota(jnp.int32, cells.shape, cells.ndim - 1)
    rolled = pltpu.roll(cells, (-by) % length, cells.ndim - 1)
    return jnp.where(lane == (0 if by < 0 else length - 1), 0.0, rolled)


def exists(gx, gy, dx, dy, count_x, count_y):
    found = []
    if dx < 0:
        found.append(gx > 0)
    if dx > 0:
        found.append(gx < count_x - 1)
    if dy < 0:
        found.append(gy > 0)
    if dy > 0:
        found.append(gy < count_y - 1)
    return functools.reduce(jnp.logical_and, found)


class Halo:
    def __init__(self, buf, send, recv, counts):
        self.buf, self.send, self.recv, self.counts = buf, send, recv, counts
        self.planes, self.rows = buf.shape[0] - 2, buf.shape[1] - 2
        self.gx, self.gy = lax.axis_index("gx"), lax.axis_index("gy")

    def clear(self):
        ends = ((self.gx == 0, 0, None), (self.gx == self.counts[0] - 1, self.planes + 1, None),
                (self.gy == 0, None, 0), (self.gy == self.counts[1] - 1, None, self.rows + 1))
        for at_end, plane, row in ends:
            @pl.when(at_end)
            def _():
                if plane is not None:
                    self.buf[plane] = jnp.zeros(self.buf.shape[1:], BF16)
                else:
                    self.buf[:, row] = jnp.zeros(self.buf.shape[:1] + self.buf.shape[2:], BF16)

    def copy(self, k):
        dx, dy = SIDES[k]

        def cut(step, size):
            if step == 0:
                return (1, 1, size)
            return (1, size + 1, 1) if step < 0 else (size, 0, 1)

        from_x, to_x, many_x = cut(dx, self.planes)
        from_y, to_y, many_y = cut(dy, self.rows)
        return pltpu.make_async_remote_copy(
            src_ref=self.buf.at[pl.ds(from_x, many_x), pl.ds(from_y, many_y)],
            dst_ref=self.buf.at[pl.ds(to_x, many_x), pl.ds(to_y, many_y)],
            send_sem=self.send.at[k],
            recv_sem=self.recv.at[k],
            device_id={"gx": self.gx + dx, "gy": self.gy + dy},
            device_id_type=MESH,
        )

    def there(self, dx, dy):
        return exists(self.gx, self.gy, dx, dy, *self.counts)

    def start(self):
        for k, (dx, dy) in enumerate(SIDES):
            @pl.when(self.there(dx, dy))
            def _():
                self.copy(k).start()

    def wait_recv(self):
        for k, (dx, dy) in enumerate(SIDES):
            @pl.when(self.there(-dx, -dy))
            def _():
                self.copy(k).wait_recv()

    def wait_send(self):
        for k, (dx, dy) in enumerate(SIDES):
            @pl.when(self.there(dx, dy))
            def _():
                self.copy(k).wait_send()


def input_rows(weights, halo_ref, x, y):
    window = halo_ref[x : x + 3, y : y + 3].reshape(weights.shape[1], halo_ref.shape[3])
    taps = nn(weights, window)
    size = taps.shape[0] // 3
    return moved(taps[:size], 1) + taps[size : 2 * size] + moved(taps[2 * size :], -1)


def filter_grad(halo_ref, taps_ref, total_ref):
    rows = [(x, y) for x in range(2) for y in range(4)]
    for at, (x, y) in enumerate(rows):
        window = halo_ref[x : x + 3, y : y + 3].reshape(CONV_ROWS, halo_ref.shape[3])
        term = nt(window, taps_ref[x, y])
        if at == 0:
            total_ref[...] = term
        else:
            total_ref[...] += term


def section(counts, d2_ref, h_ref, up_ref, c_ref, a2_ref, a1_ref, wt_ref, sort_ref,
            ig_ref, grads_ref,
            d2, d1, ub, cb, h3, up3, c3, total2, total1, send, recv):
    halo2 = Halo(d2, send.at[0], recv.at[0], counts)
    halo1 = Halo(d1, send.at[1], recv.at[1], counts)
    halou = Halo(ub, send.at[2], recv.at[2], counts)
    haloc = Halo(cb, send.at[3], recv.at[3], counts)
    barrier = pltpu.get_barrier_semaphore()
    friends = 0
    for dx, dy in SIDES:
        near = halo2.there(dx, dy)
        friends = friends + near.astype(jnp.int32)

        @pl.when(near)
        def _():
            pl.semaphore_signal(barrier, inc=1,
                                device_id={"gx": halo2.gx + dx, "gy": halo2.gy + dy}, device_id_type=MESH)
    for halo in (halo2, halo1, halou, haloc):
        halo.clear()
    d2[1:3, 1:5] = d2_ref[...]
    cb[1, 1:3] = c_ref[...]
    pl.semaphore_wait(barrier, friends)
    halo2.start()
    haloc.start()

    for x in range(2):
        for y in range(4):
            for source, taps, places in ((h_ref, h3, (0, 64, 128, 192)), (up_ref, up3, (0, 64, 192, 128))):
                cells = source[x, y]
                wide = cells.astype(F32)
                taps[x, y, places[0] : places[0] + 64] = moved(wide, -1).astype(BF16)
                taps[x, y, places[1] : places[1] + 64] = cells
                taps[x, y, places[2] : places[2] + 64] = moved(wide, 1).astype(BF16)
                taps[x, y, places[3] : places[3] + 64] = jnp.zeros_like(cells)

    halo2.wait_recv()
    for x in range(2):
        for y in range(4):
            grad = input_rows(a2_ref[...], d2, x, y)
            d1[x + 1, y + 1] = jnp.where(h_ref[x, y].astype(F32) > 0, grad, 0.0).astype(BF16)
    halo1.start()
    filter_grad(d2, h3, total2)
    haloc.wait_recv()
    for x in range(3):
        for y in range(4):
            cells = cb[x, y]
            wide = cells.astype(F32)
            c3[0, x, y] = moved(wide, -1).astype(BF16)
            c3[1, x, y] = cells
            c3[2, x, y] = moved(wide, 1).astype(BF16)

    halo1.wait_recv()
    for x in range(2):
        for y in range(4):
            grad = input_rows(a1_ref[...], d1, x, y).astype(BF16)
            ub[x + 1, y + 1] = nn(grad, sort_ref[...]).astype(BF16)
    halou.start()

    for px in range(2):
        for py in range(2):
            for pz in range(2):
                own = jnp.concatenate(
                    [ub[1 + px, 1 + 2 * row + py, :, pz * 128 : pz * 128 + 128] for row in range(2)], axis=1)
                taps, parts = [], []
                for kx in (1, 3) if px == 0 else (2, 0):
                    for ky in (1, 3) if py == 0 else (2, 0):
                        for kz in (1, 3) if pz == 0 else (2, 0):
                            sx, sy, sz = (1 if k in (1, 2) else (0 if k == 3 else 2) for k in (kx, ky, kz))
                            taps.append(16 * kx + 4 * ky + kz)
                            parts.append(jnp.concatenate([c3[sz, sx, row + sy] for row in range(2)], axis=1))
                result = nt(own, jnp.concatenate(parts, axis=0)).astype(BF16)
                for at, tap in enumerate(taps):
                    grads_ref[tap * 64 : tap * 64 + 64] = result[:, at * 128 : at * 128 + 128]

    filter_grad(d1, up3, total1)
    first, second, third = (TCONV_ROWS + CONV_ROWS * at for at in range(3))
    grads_ref[first : first + CONV_ROWS] = total2[:, :128].astype(BF16)
    grads_ref[second : second + CONV_ROWS] = total1[:, :128].astype(BF16)
    grads_ref[third : third + CONV_ROWS] = (total2[:, 128:] + total1[:, 128:]).astype(BF16)
    grads_ref[third + CONV_ROWS :] = jnp.zeros((ROWS - third - CONV_ROWS, 128), BF16)

    halou.wait_recv()
    sums = []
    for half in range(2):
        around = jnp.concatenate(
            [ub[:, 2 * row : 2 * row + 4, :, half * 128 : half * 128 + 128].reshape(1024, 128) for row in range(2)],
            axis=1)
        sums.append(nn(wt_ref[half], around))
    even, odd = sums
    for row in range(2):
        lanes = slice(row * 128, row * 128 + 128)
        ig_ref[row] = (even[:128, lanes] + moved(even[128:, lanes], 1)
                       + odd[128:, lanes] + moved(odd[:128, lanes], -1)).astype(BF16)
    for halo in (halo2, halo1, halou, haloc):
        halo.wait_send()


def sum_all(grads_ref, out_ref, held, got0, got1, got2, got3, own1, own2, own3,
            core_send, core_recv, send, recv):
    gx, gy = lax.axis_index("gx"), lax.axis_index("gy")
    place = {"x": gx % 4, "z": gx // 4 % 4, "y": gx // 16 * 2 + gy // 2}
    core = gy % 2

    def device(axis=None, at=None, which=core):
        spot = dict(place)
        if axis is not None:
            spot[axis] = at
        return {"gx": spot["y"] // 2 * 16 + spot["z"] * 4 + spot["x"], "gy": spot["y"] % 2 * 2 + which}

    barrier = pltpu.get_barrier_semaphore()
    peers = [device(which=1 - core)]
    for axis in "xyz":
        for j in (1, 2, 3):
            peers.append(device(axis, (place[axis] + j) % 4))
    for peer in peers:
        pl.semaphore_signal(barrier, inc=1, device_id=peer, device_id_type=MESH)
    pl.semaphore_wait(barrier, len(peers))

    def rows_at(start, size):
        return pl.ds(pl.multiple_of(start, 16), size)

    def remote(src, dst, send_sem, recv_sem, peer):
        return pltpu.make_async_remote_copy(src_ref=src, dst_ref=dst, send_sem=send_sem, recv_sem=recv_sem,
                                            device_id=peer, device_id_type=MESH)

    swap = remote(grads_ref.at[rows_at((1 - core) * HALF, HALF)], got0, core_send.at[0], core_recv.at[0],
                  device(which=1 - core))
    swap.start()
    swap.wait()
    held[...] = (grads_ref[rows_at(core * HALF, HALF)].astype(F32) + got0[...].astype(F32)).astype(BF16)

    orders = ("xyz", "yzx", "zxy")
    sources = [held.at[pl.ds(PART * part, PART)] for part in range(3)]
    base = [core * HALF + PART * part for part in range(3)]
    bases = [list(base)]
    for stage, (got, own) in enumerate(((got1, own1), (got2, own2), (got3, own3))):
        size = PART // 4 ** (stage + 1)
        copies = []
        for part in range(3):
            axis = orders[part][stage]
            for j in (1, 2, 3):
                to = (place[axis] + j) % 4
                copies.append(remote(sources[part].at[rows_at(to * size, size)], got.at[part, j - 1],
                                     send.at[stage, part, j - 1], recv.at[stage, part, j - 1], device(axis, to)))
        for copy in copies:
            copy.start()
        for part in range(3):
            here = place[orders[part][stage]]
            for j in range(3):
                copies[part * 3 + j].wait_recv()
            total = sources[part][rows_at(here * size, size)].astype(F32)
            for j in range(3):
                total = total + got[part, j].astype(F32)
            own[part] = total.astype(BF16)
            base[part] = base[part] + here * size
        for copy in copies:
            copy.wait_send()
        sources = [own.at[part] for part in range(3)]
        bases.append(list(base))

    for part in range(3):
        out_ref[rows_at(base[part], PART // 64)] = own3[part]
    for stage in (2, 1, 0):
        size = PART // 4 ** (stage + 1)
        copies = []
        for part in range(3):
            axis = orders[part][stage]
            block = out_ref.at[rows_at(bases[stage + 1][part], size)]
            for j in (1, 2, 3):
                copies.append(remote(block, block, send.at[5 - stage, part, j - 1], recv.at[5 - stage, part, j - 1],
                                     device(axis, (place[axis] + j) % 4)))
        for copy in copies:
            copy.start()
        for copy in copies:
            copy.wait()
    block = out_ref.at[rows_at(core * HALF, HALF)]
    swap = remote(block, block, core_send.at[1], core_recv.at[1], device(which=1 - core))
    swap.start()
    swap.wait()


def widen(scale, rows_ref, tconv_ref, one_ref, two_ref):
    for tap in range(64):
        tconv_ref[tap] = rows_ref[tap * 64 : tap * 64 + 64].astype(F32) * scale
    for a in range(3):
        for b in range(3):
            at = ((2 - a) * 3 + 2 - b) * 64
            first, second, third = (TCONV_ROWS + CONV_ROWS * n + at for n in range(3))
            low2 = rows_ref[first : first + 64].astype(F32) * scale
            low1 = rows_ref[second : second + 64].astype(F32) * scale
            high = rows_ref[third : third + 64].astype(F32) * scale
            tap = 9 * a + 3 * b
            two_ref[tap] = low2[:, :64]
            two_ref[tap + 1] = low2[:, 64:]
            two_ref[tap + 2] = high[:, :64]
            one_ref[tap] = low1[:, :64]
            one_ref[tap + 1] = low1[:, 64:]
            one_ref[tap + 2] = high[:, 64:]


def conv_matrix(weight):
    taps = weight.reshape(3, 3, 3, 64, 64)[::-1, ::-1]
    return taps.transpose(2, 4, 0, 1, 3).reshape(192, 576)


def shards(counts, coarse_input, upsampled, hidden_one, hidden_two, cotangent,
           tconv_weight, conv_one_weight, conv_two_weight):
    channels, planes, across, length = cotangent.shape
    scale = 1.0 / math.sqrt(planes * counts[0] * across * counts[1] * length)
    delta_two = jnp.where(hidden_two > 0, cotangent, jnp.zeros_like(cotangent))
    by_row = lambda cells: cells.transpose(1, 2, 0, 3)
    taps = tconv_weight.reshape(4, 4, 4, 64, 128)
    wt = jnp.stack([
        jnp.stack([taps[:, :, low], taps[:, :, low + 2]]).transpose(0, 4, 1, 2, 3).reshape(256, 1024)
        for low in (1, 0)])
    at = jnp.arange(length)
    sort = (at[:, None] == (at % 128 * 2 + at // 128)[None, :]).astype(BF16)
    vmem = pl.BlockSpec(memory_space=pltpu.VMEM)
    row = (channels, length)
    input_grad, grads = pl.pallas_call(
        functools.partial(section, counts),
        out_shape=(jax.ShapeDtypeStruct((2, 128, 128), BF16), jax.ShapeDtypeStruct((ROWS, 128), BF16)),
        in_specs=[vmem] * 8,
        out_specs=(vmem, vmem),
        scratch_shapes=[
            pltpu.VMEM((4, 6) + row, BF16),
            pltpu.VMEM((4, 6) + row, BF16),
            pltpu.VMEM((4, 6) + row, BF16),
            pltpu.VMEM((3, 4, 128, 128), BF16),
            pltpu.VMEM((2, 4, 256, length), BF16),
            pltpu.VMEM((2, 4, 256, length), BF16),
            pltpu.VMEM((3, 3, 4, 128, 128), BF16),
            pltpu.VMEM((CONV_ROWS, 256), F32),
            pltpu.VMEM((CONV_ROWS, 256), F32),
            pltpu.SemaphoreType.DMA((4, 8)),
            pltpu.SemaphoreType.DMA((4, 8)),
        ],
        compiler_params=pltpu.CompilerParams(collective_id=0, has_side_effects=True, vmem_limit_bytes=VMEM_BYTES),
    )(by_row(delta_two), by_row(hidden_one), by_row(upsampled), coarse_input[:, 0].transpose(1, 0, 2),
      conv_matrix(conv_two_weight), conv_matrix(conv_one_weight), wt, sort)

    total = pl.pallas_call(
        sum_all,
        out_shape=jax.ShapeDtypeStruct((ROWS, 128), BF16),
        in_specs=[vmem],
        out_specs=vmem,
        scratch_shapes=[
            pltpu.VMEM((HALF, 128), BF16),
            pltpu.VMEM((HALF, 128), BF16),
            pltpu.VMEM((3, 3, PART // 4, 128), BF16),
            pltpu.VMEM((3, 3, PART // 16, 128), BF16),
            pltpu.VMEM((3, 3, PART // 64, 128), BF16),
            pltpu.VMEM((3, PART // 4, 128), BF16),
            pltpu.VMEM((3, PART // 16, 128), BF16),
            pltpu.VMEM((3, PART // 64, 128), BF16),
            pltpu.SemaphoreType.DMA((2,)),
            pltpu.SemaphoreType.DMA((2,)),
            pltpu.SemaphoreType.DMA((6, 3, 3)),
            pltpu.SemaphoreType.DMA((6, 3, 3)),
        ],
        compiler_params=pltpu.CompilerParams(collective_id=1, has_side_effects=True, vmem_limit_bytes=VMEM_BYTES),
    )(grads)

    tconv_grad, one_grad, two_grad = pl.pallas_call(
        functools.partial(widen, scale),
        out_shape=(jax.ShapeDtypeStruct((64, 64, 128), F32), jax.ShapeDtypeStruct((27, 64, 64), F32),
                   jax.ShapeDtypeStruct((27, 64, 64), F32)),
        in_specs=[vmem],
        out_specs=(vmem, vmem, vmem),
        compiler_params=pltpu.CompilerParams(vmem_limit_bytes=VMEM_BYTES),
    )(total)
    return input_grad.transpose(1, 0, 2)[:, None], tconv_grad, one_grad, two_grad


def solution(mesh):
    cells = P(None, "gx", "gy", None)
    return jax.shard_map(
        functools.partial(shards, (mesh.shape["gx"], mesh.shape["gy"])),
        mesh=mesh,
        in_specs=(cells,) * 5 + (P(),) * 3,
        out_specs=(cells, P(), P(), P()),
        check_vma=False,
    )
```

```python
import functools
import math

import jax
import jax.numpy as jnp
from jax import lax
from jax.experimental import pallas as pl
from jax.experimental.pallas import tpu as pltpu
from jax.sharding import PartitionSpec as P

BF16 = jnp.bfloat16
F32 = jnp.float32
MESH = pl.DeviceIdType.MESH
SIDES = [(dx, dy) for dx in (-1, 0, 1) for dy in (-1, 0, 1) if dx or dy]
VMEM_BYTES = 56 * 1024 * 1024

CONV_ROWS = 576
MIXED_ROWS = CONV_ROWS // 2
PART = 1024
HALF = 3 * PART
ROWS = 2 * HALF
CLASS_ROWS = 512
ORDERS = ("xyz", "yzx", "zxy")


def nn(a, b):
    return lax.dot_general(a, b, (((1,), (0,)), ((), ())), preferred_element_type=F32)


def nt(a, b):
    return lax.dot_general(a, b, (((1,), (1,)), ((), ())), preferred_element_type=F32)


def moved(cells, by):
    length = cells.shape[-1]
    lane = lax.broadcasted_iota(jnp.int32, cells.shape, cells.ndim - 1)
    rolled = pltpu.roll(cells, (-by) % length, cells.ndim - 1)
    return jnp.where(lane == (0 if by < 0 else length - 1), 0.0, rolled)


def exists(gx, gy, dx, dy, count_x, count_y):
    found = []
    if dx < 0:
        found.append(gx > 0)
    if dx > 0:
        found.append(gx < count_x - 1)
    if dy < 0:
        found.append(gy > 0)
    if dy > 0:
        found.append(gy < count_y - 1)
    return functools.reduce(jnp.logical_and, found)


class Halo:
    def __init__(self, buf, send, recv, counts):
        self.buf, self.send, self.recv, self.counts = buf, send, recv, counts
        self.planes, self.rows = buf.shape[0] - 2, buf.shape[1] - 2
        self.gx, self.gy = lax.axis_index("gx"), lax.axis_index("gy")

    def clear(self):
        ends = ((self.gx == 0, 0, None), (self.gx == self.counts[0] - 1, self.planes + 1, None),
                (self.gy == 0, None, 0), (self.gy == self.counts[1] - 1, None, self.rows + 1))
        for at_end, plane, row in ends:
            @pl.when(at_end)
            def _():
                if plane is not None:
                    self.buf[plane] = jnp.zeros(self.buf.shape[1:], BF16)
                else:
                    self.buf[:, row] = jnp.zeros(self.buf.shape[:1] + self.buf.shape[2:], BF16)

    def copy(self, k):
        dx, dy = SIDES[k]

        def cut(step, size):
            if step == 0:
                return (1, 1, size)
            return (1, size + 1, 1) if step < 0 else (size, 0, 1)

        from_x, to_x, many_x = cut(dx, self.planes)
        from_y, to_y, many_y = cut(dy, self.rows)
        return pltpu.make_async_remote_copy(
            src_ref=self.buf.at[pl.ds(from_x, many_x), pl.ds(from_y, many_y)],
            dst_ref=self.buf.at[pl.ds(to_x, many_x), pl.ds(to_y, many_y)],
            send_sem=self.send.at[k],
            recv_sem=self.recv.at[k],
            device_id={"gx": self.gx + dx, "gy": self.gy + dy},
            device_id_type=MESH,
        )

    def there(self, dx, dy):
        return exists(self.gx, self.gy, dx, dy, *self.counts)

    def start(self, steps=(-1, 0, 1)):
        for k, (dx, dy) in enumerate(SIDES):
            if dx not in steps:
                continue

            @pl.when(self.there(dx, dy))
            def _():
                self.copy(k).start()

    def wait_recv(self):
        for k, (dx, dy) in enumerate(SIDES):
            @pl.when(self.there(-dx, -dy))
            def _():
                self.copy(k).wait_recv()

    def wait_send(self):
        for k, (dx, dy) in enumerate(SIDES):
            @pl.when(self.there(dx, dy))
            def _():
                self.copy(k).wait_send()


def input_rows(weights, halo_ref, x, y):
    window = halo_ref[x : x + 3, y : y + 3].reshape(weights.shape[1], halo_ref.shape[3])
    taps = nn(weights, window)
    size = taps.shape[0] // 3
    return moved(taps[:size], 1) + taps[size : 2 * size] + moved(taps[2 * size :], -1)


def filter_grad(halo_ref, taps_ref):
    rows = [(x, y) for x in range(2) for y in range(4)]
    windows = [halo_ref[x : x + 3, y : y + 3].reshape(CONV_ROWS, halo_ref.shape[3]) for x, y in rows]
    return nt(jnp.concatenate(windows, axis=1), jnp.concatenate([taps_ref[x, y] for x, y in rows], axis=1))


def conv_matrix(weight_ref, rows_ref, matrix_ref):
    rows_ref[:, 192:] = jnp.zeros((CONV_ROWS, 64), BF16)
    for a in range(3):
        for b in range(3):
            at = ((2 - a) * 3 + 2 - b) * 64
            for c in range(3):
                rows_ref[at : at + 64, c * 64 : c * 64 + 64] = weight_ref[9 * a + 3 * b + c]
    matrix_ref[...] = rows_ref[...].T[:192]


def tap_choices(parity):
    return ((2, 1), (0, 2)) if parity else ((1, 1), (3, 0))


def class_grad(ub, c3, px, py, pz):
    own = jnp.concatenate(
        [ub[1 + px, 1 + 2 * row + py, :, pz * 128 : pz * 128 + 128] for row in range(2)], axis=1)
    parts = []
    for sx in (1, 2 * px):
        for _, sy in tap_choices(py):
            for _, sz in tap_choices(pz):
                parts.append(jnp.concatenate([c3[sz, sx, row + sy] for row in range(2)], axis=1))
    return nt(own, jnp.concatenate(parts, axis=0))


def section(counts, c_ref, up_ref, h_ref, h_two_ref, g_ref, wt_ref, w1_ref, w2_ref, ig_ref, out_ref,
            d2, d1, ub, cb, h3, up3, c3, rows, a2, a1, sort, pack, away, away_mixed, got0, got0_mixed,
            held, got1, got2, got3, own1, own2, own3,
            halo_send, halo_recv, core_send, core_recv, send, recv):
    gx, gy = lax.axis_index("gx"), lax.axis_index("gy")
    place = {"x": gx % 4, "z": gx // 4 % 4, "y": gx // 16 * 2 + gy // 2}
    core = gy % 2

    def device(axis, at):
        spot = dict(place)
        spot[axis] = at
        return {"gx": spot["y"] // 2 * 16 + spot["z"] * 4 + spot["x"], "gy": spot["y"] % 2 * 2 + core}

    sibling = {"gx": gx, "gy": gy - core + 1 - core}

    def remote(src, dst, send_sem, recv_sem, peer):
        return pltpu.make_async_remote_copy(src_ref=src, dst_ref=dst, send_sem=send_sem, recv_sem=recv_sem,
                                            device_id=peer, device_id_type=MESH)

    halo2, halo1, halou, haloc = (
        Halo(buf, halo_send.at[at], halo_recv.at[at], counts) for at, buf in enumerate((d2, d1, ub, cb)))
    barrier = pltpu.get_barrier_semaphore()
    peers = [sibling] + [device(axis, (place[axis] + j) % 4) for axis in "xyz" for j in (1, 2, 3)]
    for peer in peers:
        pl.semaphore_signal(barrier, inc=1, device_id=peer, device_id_type=MESH)
    friends = len(peers)
    for dx, dy in SIDES:
        near = halo2.there(dx, dy)
        friends = friends + near.astype(jnp.int32)

        @pl.when(near)
        def _():
            pl.semaphore_signal(barrier, inc=1, device_id={"gx": gx + dx, "gy": gy + dy}, device_id_type=MESH)
    for halo in (halo2, halo1, halou, haloc):
        halo.clear()
    for x in range(2):
        masked = jnp.where(h_two_ref[:, x].astype(F32) > 0, g_ref[:, x].astype(F32), 0.0).astype(BF16)
        d2[x + 1, 1:5] = jnp.swapaxes(masked, 0, 1)
    cb[1, 1:3] = jnp.swapaxes(c_ref[:, 0], 0, 1)
    pl.semaphore_wait(barrier, friends)
    halo2.start()
    haloc.start()

    conv_matrix(w2_ref, rows, a2)
    for source, taps, places in ((h_ref, h3, (0, 64, 128, 192)), (up_ref, up3, (0, 64, 192, 128))):
        for x in range(2):
            plane = jnp.swapaxes(source[:, x], 0, 1)
            for y in range(4):
                cells = plane[y]
                wide = cells.astype(F32)
                taps[x, y, places[0] : places[0] + 64] = moved(wide, -1).astype(BF16)
                taps[x, y, places[1] : places[1] + 64] = cells
                taps[x, y, places[2] : places[2] + 64] = moved(wide, 1).astype(BF16)
                taps[x, y, places[3] : places[3] + 64] = jnp.zeros_like(cells)

    halo2.wait_recv()
    for x in range(2):
        for y in range(4):
            grad = input_rows(a2[...], d2, x, y)
            d1[x + 1, y + 1] = jnp.where(h3[x, y, 64:128].astype(F32) > 0, grad, 0.0).astype(BF16)
        halo1.start((-1,) if x == 0 else (0, 1))

    conv_matrix(w1_ref, rows, a1)
    from_z = lax.broadcasted_iota(jnp.int32, sort.shape, 0)
    to_z = lax.broadcasted_iota(jnp.int32, sort.shape, 1)
    sort[...] = jnp.where(from_z == to_z % 128 * 2 + to_z // 128, 1.0, 0.0).astype(BF16)
    total2 = filter_grad(d2, h3)
    pack[0, :CONV_ROWS] = total2[:, :128]
    pack[0, CONV_ROWS : CONV_ROWS + MIXED_ROWS] = total2[:MIXED_ROWS, 128:]
    pack[1, CONV_ROWS : CONV_ROWS + MIXED_ROWS] = total2[MIXED_ROWS:, 128:]
    for half in range(2):
        pack[half, CONV_ROWS + MIXED_ROWS :] = jnp.zeros((PART - CONV_ROWS - MIXED_ROWS, 128), F32)
    haloc.wait_recv()
    for x in range(3):
        for y in range(4):
            cells = cb[x, y]
            wide = cells.astype(F32)
            c3[0, x, y] = moved(wide, -1).astype(BF16)
            c3[1, x, y] = cells
            c3[2, x, y] = moved(wide, 1).astype(BF16)

    halo1.wait_recv()
    for x in range(2):
        plane = jnp.concatenate([input_rows(a1[...], d1, x, y).astype(BF16) for y in range(4)], axis=0)
        ub[x + 1, 1:5] = nn(plane, sort[...]).astype(BF16).reshape(4, 64, 256)
        halou.start((-1,) if x == 0 else (0, 1))

    total1 = filter_grad(d1, up3)
    pack[1, :CONV_ROWS] = total1[:, :128]
    pack[0, CONV_ROWS : CONV_ROWS + MIXED_ROWS] += total1[:MIXED_ROWS, 128:]
    pack[1, CONV_ROWS : CONV_ROWS + MIXED_ROWS] += total1[MIXED_ROWS:, 128:]
    away_mixed[...] = pack[1 - core].astype(BF16)
    mixed = remote(away_mixed, got0_mixed, core_send.at[4], core_recv.at[4], sibling)
    mixed.start()

    classes = [(py, pz) for py in range(2) for pz in range(2)]
    swaps = []
    for at, (py, pz) in enumerate(classes):
        result = class_grad(ub, c3, 1 - core, py, pz).astype(BF16)
        for n in range(8):
            away[at, n * 64 : n * 64 + 64] = result[:, n * 128 : n * 128 + 128]
        swaps.append(remote(away.at[at], got0.at[at], core_send.at[at], core_recv.at[at], sibling))
        swaps[-1].start()
    for at, (py, pz) in enumerate(classes):
        result = class_grad(ub, c3, core, py, pz)
        swaps[at].wait_recv()
        for n in range(8):
            to = at * CLASS_ROWS + n * 64
            held[to : to + 64] = (
                result[:, n * 128 : n * 128 + 128] + got0[at, n * 64 : n * 64 + 64].astype(F32)).astype(BF16)
    mixed.wait_recv()
    held[2 * PART :] = (pack[core] + got0_mixed[...].astype(F32)).astype(BF16)

    def rows_at(start, size):
        return pl.ds(pl.multiple_of(start, 16), size)

    sources = [held.at[pl.ds(PART * part, PART)] for part in range(3)]
    bases = [[core * HALF + PART * part for part in range(3)]]
    for stage, (got, own) in enumerate(((got1, own1), (got2, own2), (got3, own3))):
        size = PART // 4 ** (stage + 1)
        copies = []
        for part in range(3):
            axis = ORDERS[part][stage]
            for j in (1, 2, 3):
                to = (place[axis] + j) % 4
                copies.append(remote(sources[part].at[rows_at(to * size, size)], got.at[part, j - 1],
                                     send.at[stage, part, j - 1], recv.at[stage, part, j - 1], device(axis, to)))
        for copy in copies:
            copy.start()
        if stage == 0:
            halou.wait_recv()
            input_grad(ub, wt_ref, ig_ref)
        base = []
        for part in range(3):
            here = place[ORDERS[part][stage]]
            for j in range(3):
                copies[part * 3 + j].wait_recv()
            total = sources[part][rows_at(here * size, size)].astype(F32)
            for j in range(3):
                total = total + got[part, j].astype(F32)
            own[part] = total.astype(BF16)
            base.append(bases[-1][part] + here * size)
        for copy in copies:
            copy.wait_send()
        sources = [own.at[part] for part in range(3)]
        bases.append(base)

    for part in range(3):
        out_ref[rows_at(bases[3][part], PART // 64)] = own3[part]
    sent, shares = [], []
    for stage in (2, 1, 0):
        size = PART // 4 ** (stage + 1)
        copies = []
        for part in range(3):
            axis = ORDERS[part][stage]
            block = out_ref.at[rows_at(bases[stage + 1][part], size)]
            for j in (1, 2, 3):
                copies.append(remote(block, block, send.at[5 - stage, part, j - 1], recv.at[5 - stage, part, j - 1],
                                     device(axis, (place[axis] + j) % 4)))
        for copy in copies:
            copy.start()

        def share(part, start, at):
            block = out_ref.at[rows_at(start, size)]
            shares.append(remote(block, block, core_send.at[5 + at], core_recv.at[5 + at], sibling))
            shares[-1].start()

        if stage == 0:
            for part in range(3):
                share(part, bases[1][part], part)
        for j in (1, 2, 3):
            for part in range(3):
                copies[part * 3 + j - 1].wait_recv()
                if stage == 0:
                    from_place = (place[ORDERS[part][0]] + 4 - j) % 4
                    share(part, bases[0][part] + from_place * size, j * 3 + part)
        sent += copies
    for copy in shares:
        copy.wait_recv()
    for copy in sent + shares + swaps + [mixed]:
        copy.wait_send()
    for halo in (halo2, halo1, halou, haloc):
        halo.wait_send()


def input_grad(ub, wt_ref, ig_ref):
    sums = []
    for half in range(2):
        around = jnp.concatenate(
            [ub[:, 2 * row : 2 * row + 4, :, half * 128 : half * 128 + 128].reshape(1024, 128) for row in range(2)],
            axis=1)
        filters = jnp.concatenate(
            [jnp.concatenate([wt_ref[4 * at + kz] for at in range(16)], axis=0) for kz in (1 - half, 3 - half)], axis=1)
        sums.append(lax.dot_general(filters, around, (((0,), (0,)), ((), ())), preferred_element_type=F32))
    even, odd = sums
    for row in range(2):
        lanes = slice(row * 128, row * 128 + 128)
        ig_ref[row] = (even[:128, lanes] + moved(even[128:, lanes], 1)
                       + odd[128:, lanes] + moved(odd[:128, lanes], -1)).astype(BF16)


def widen(scale, rows_ref, tconv_ref, one_ref, two_ref):
    for px in range(2):
        for at in range(4):
            py, pz = at // 2, at % 2
            n = 0
            for kx, _ in tap_choices(px):
                for ky, _ in tap_choices(py):
                    for kz, _ in tap_choices(pz):
                        start = px * HALF + at * CLASS_ROWS + n * 64
                        tconv_ref[16 * kx + 4 * ky + kz] = rows_ref[start : start + 64].astype(F32) * scale
                        n += 1

    def mixed(start, size):
        half, inside = start // MIXED_ROWS, start % MIXED_ROWS
        at = half * HALF + 2 * PART + CONV_ROWS + inside
        many = min(size, MIXED_ROWS - inside)
        found = rows_ref[at : at + many].astype(F32)
        return found if many == size else jnp.concatenate([found, mixed(start + many, size - many)], axis=0)

    for a in range(3):
        for b in range(3):
            at = ((2 - a) * 3 + 2 - b) * 64
            low2 = rows_ref[2 * PART + at : 2 * PART + at + 64].astype(F32) * scale
            low1 = rows_ref[HALF + 2 * PART + at : HALF + 2 * PART + at + 64].astype(F32) * scale
            high = mixed(at, 64) * scale
            tap = 9 * a + 3 * b
            two_ref[tap] = low2[:, :64]
            two_ref[tap + 1] = low2[:, 64:]
            two_ref[tap + 2] = high[:, :64]
            one_ref[tap] = low1[:, :64]
            one_ref[tap + 1] = low1[:, 64:]
            one_ref[tap + 2] = high[:, 64:]


def shards(counts, coarse_input, upsampled, hidden_one, hidden_two, cotangent,
           tconv_weight, conv_one_weight, conv_two_weight):
    channels, planes, across, length = cotangent.shape
    scale = 1.0 / math.sqrt(planes * counts[0] * across * counts[1] * length)
    vmem = pl.BlockSpec(memory_space=pltpu.VMEM)
    haloed = pltpu.VMEM((4, 6, channels, length), BF16)
    shifted = pltpu.VMEM((2, 4, 256, length), BF16)
    input_grad, total = pl.pallas_call(
        functools.partial(section, counts),
        out_shape=(jax.ShapeDtypeStruct((2, 128, 128), BF16), jax.ShapeDtypeStruct((ROWS, 128), BF16)),
        in_specs=[vmem] * 8,
        out_specs=(vmem, vmem),
        scratch_shapes=[
            haloed, haloed, haloed, pltpu.VMEM((3, 4, 128, 128), BF16),
            shifted, shifted, pltpu.VMEM((3, 3, 4, 128, 128), BF16),
            pltpu.VMEM((CONV_ROWS, 256), BF16), pltpu.VMEM((192, CONV_ROWS), BF16), pltpu.VMEM((192, CONV_ROWS), BF16),
            pltpu.VMEM((length, length), BF16), pltpu.VMEM((2, PART, 128), F32),
            pltpu.VMEM((4, CLASS_ROWS, 128), BF16), pltpu.VMEM((PART, 128), BF16),
            pltpu.VMEM((4, CLASS_ROWS, 128), BF16), pltpu.VMEM((PART, 128), BF16),
            pltpu.VMEM((HALF, 128), BF16),
            pltpu.VMEM((3, 3, PART // 4, 128), BF16),
            pltpu.VMEM((3, 3, PART // 16, 128), BF16),
            pltpu.VMEM((3, 3, PART // 64, 128), BF16),
            pltpu.VMEM((3, PART // 4, 128), BF16),
            pltpu.VMEM((3, PART // 16, 128), BF16),
            pltpu.VMEM((3, PART // 64, 128), BF16),
            pltpu.SemaphoreType.DMA((4, 8)), pltpu.SemaphoreType.DMA((4, 8)),
            pltpu.SemaphoreType.DMA((17,)), pltpu.SemaphoreType.DMA((17,)),
            pltpu.SemaphoreType.DMA((6, 3, 3)), pltpu.SemaphoreType.DMA((6, 3, 3)),
        ],
        compiler_params=pltpu.CompilerParams(collective_id=0, has_side_effects=True, vmem_limit_bytes=VMEM_BYTES),
    )(coarse_input, upsampled, hidden_one, hidden_two, cotangent, tconv_weight, conv_one_weight, conv_two_weight)

    tconv_grad, one_grad, two_grad = pl.pallas_call(
        functools.partial(widen, scale),
        out_shape=(jax.ShapeDtypeStruct((64, 64, 128), F32), jax.ShapeDtypeStruct((27, 64, 64), F32),
                   jax.ShapeDtypeStruct((27, 64, 64), F32)),
        in_specs=[vmem],
        out_specs=(vmem, vmem, vmem),
        compiler_params=pltpu.CompilerParams(vmem_limit_bytes=VMEM_BYTES),
    )(total)
    return input_grad.transpose(1, 0, 2)[:, None], tconv_grad, one_grad, two_grad


def solution(mesh):
    cells = P(None, "gx", "gy", None)
    return jax.shard_map(
        functools.partial(shards, (mesh.shape["gx"], mesh.shape["gy"])),
        mesh=mesh,
        in_specs=(cells,) * 5 + (P(),) * 3,
        out_specs=(cells, P(), P(), P()),
        check_vma=False,
    )
```

```python
import functools
import math

import jax
import jax.numpy as jnp
from jax import lax
from jax.experimental import pallas as pl
from jax.experimental.pallas import tpu as pltpu
from jax.sharding import PartitionSpec as P

BF16 = jnp.bfloat16
F32 = jnp.float32
MESH = pl.DeviceIdType.MESH
SIDES = [(dx, dy) for dx in (-1, 0, 1) for dy in (-1, 0, 1) if dx or dy]
VMEM_BYTES = 56 * 1024 * 1024

CONV_ROWS = 576
MIXED_ROWS = CONV_ROWS // 2
PART = 1024
HALF = 3 * PART
ROWS = 2 * HALF
CLASS_ROWS = 512
QUARTER = PART // 4
PIECE = QUARTER // 16
ORDERS = ("xyz", "yzx", "zxy")


def nn(a, b):
    return lax.dot_general(a, b, (((1,), (0,)), ((), ())), preferred_element_type=F32)


def nt(a, b):
    return lax.dot_general(a, b, (((1,), (1,)), ((), ())), preferred_element_type=F32)


def moved(cells, by):
    length = cells.shape[-1]
    lane = lax.broadcasted_iota(jnp.int32, cells.shape, cells.ndim - 1)
    rolled = pltpu.roll(cells, (-by) % length, cells.ndim - 1)
    return jnp.where(lane == (0 if by < 0 else length - 1), 0.0, rolled)


def exists(gx, gy, dx, dy, count_x, count_y):
    found = []
    if dx < 0:
        found.append(gx > 0)
    if dx > 0:
        found.append(gx < count_x - 1)
    if dy < 0:
        found.append(gy > 0)
    if dy > 0:
        found.append(gy < count_y - 1)
    return functools.reduce(jnp.logical_and, found)


class Halo:
    def __init__(self, buf, send, recv, counts):
        self.buf, self.send, self.recv, self.counts = buf, send, recv, counts
        self.planes, self.rows = buf.shape[0] - 2, buf.shape[1] - 2
        self.gx, self.gy = lax.axis_index("gx"), lax.axis_index("gy")

    def clear(self):
        ends = ((self.gx == 0, 0, None), (self.gx == self.counts[0] - 1, self.planes + 1, None),
                (self.gy == 0, None, 0), (self.gy == self.counts[1] - 1, None, self.rows + 1))
        for at_end, plane, row in ends:
            @pl.when(at_end)
            def _():
                if plane is not None:
                    self.buf[plane] = jnp.zeros(self.buf.shape[1:], BF16)
                else:
                    self.buf[:, row] = jnp.zeros(self.buf.shape[:1] + self.buf.shape[2:], BF16)

    def copy(self, k):
        dx, dy = SIDES[k]

        def cut(step, size):
            if step == 0:
                return (1, 1, size)
            return (1, size + 1, 1) if step < 0 else (size, 0, 1)

        from_x, to_x, many_x = cut(dx, self.planes)
        from_y, to_y, many_y = cut(dy, self.rows)
        return pltpu.make_async_remote_copy(
            src_ref=self.buf.at[pl.ds(from_x, many_x), pl.ds(from_y, many_y)],
            dst_ref=self.buf.at[pl.ds(to_x, many_x), pl.ds(to_y, many_y)],
            send_sem=self.send.at[k],
            recv_sem=self.recv.at[k],
            device_id={"gx": self.gx + dx, "gy": self.gy + dy},
            device_id_type=MESH,
        )

    def there(self, dx, dy):
        return exists(self.gx, self.gy, dx, dy, *self.counts)

    def start(self, steps=(-1, 0, 1)):
        for k, (dx, dy) in enumerate(SIDES):
            if dx not in steps:
                continue

            @pl.when(self.there(dx, dy))
            def _():
                self.copy(k).start()

    def wait_recv(self):
        for k, (dx, dy) in enumerate(SIDES):
            @pl.when(self.there(-dx, -dy))
            def _():
                self.copy(k).wait_recv()

    def wait_send(self):
        for k, (dx, dy) in enumerate(SIDES):
            @pl.when(self.there(dx, dy))
            def _():
                self.copy(k).wait_send()


def before(cells):
    half = cells.shape[-1] // 2
    return jnp.concatenate([moved(cells[..., half:], -1), cells[..., :half]], axis=-1)


def after(cells):
    half = cells.shape[-1] // 2
    return jnp.concatenate([cells[..., half:], moved(cells[..., :half], 1)], axis=-1)


def input_rows(weights, halo_ref, x, y):
    window = halo_ref[x : x + 3, y : y + 3].reshape(weights.shape[1], halo_ref.shape[3])
    taps = nn(weights, window)
    size = taps.shape[0] // 3
    return after(taps[:size]) + taps[size : 2 * size] + before(taps[2 * size :])


def filter_grad(halo_ref, taps_ref):
    rows = [(x, y) for x in range(2) for y in range(4)]
    windows = [halo_ref[x : x + 3, y : y + 3].reshape(CONV_ROWS, halo_ref.shape[3]) for x, y in rows]
    return nt(jnp.concatenate(windows, axis=1), jnp.concatenate([taps_ref[x, y] for x, y in rows], axis=1))


def conv_matrix(weight_ref, rows_ref, matrix_ref):
    rows_ref[:, 192:] = jnp.zeros((CONV_ROWS, 64), BF16)
    for a in range(3):
        for b in range(3):
            at = ((2 - a) * 3 + 2 - b) * 64
            for c in range(3):
                rows_ref[at : at + 64, c * 64 : c * 64 + 64] = weight_ref[9 * a + 3 * b + c]
    matrix_ref[...] = rows_ref[...].T[:192]


def tap_choices(parity):
    return ((2, 1), (0, 2)) if parity else ((1, 1), (3, 0))


def class_grad(ub, c3, px, py, pz):
    own = jnp.concatenate(
        [ub[1 + px, 1 + 2 * row + py, :, pz * 128 : pz * 128 + 128] for row in range(2)], axis=1)
    parts = []
    for sx in (1, 2 * px):
        for _, sy in tap_choices(py):
            for _, sz in tap_choices(pz):
                parts.append(jnp.concatenate([c3[sz, sx, row + sy] for row in range(2)], axis=1))
    return nt(own, jnp.concatenate(parts, axis=0))


def section(counts, c_any, up_any, h_any, h_two_any, g_any, wt_any, w1_any, w2_any, ig_ref, out_ref,
            c_ref, up_ref, h_ref, h_two_ref, g_ref, wt_ref, w1_ref, w2_ref,
            d2, d1, ub, cb, h3, up3, c3, rows, a2, a1, sort, pack, away, away_mixed, got0, got0_mixed,
            held, got1, got2, own1,
            load, halo_send, halo_recv, core_send, core_recv, ring_send, ring_recv, plane_send, plane_recv):
    loads = {}
    for at, (name, source, to) in enumerate((
            ("g", g_any, g_ref), ("h_two", h_two_any, h_two_ref), ("c", c_any, c_ref), ("w2", w2_any, w2_ref),
            ("h", h_any, h_ref), ("up", up_any, up_ref), ("w1", w1_any, w1_ref), ("wt", wt_any, wt_ref))):
        loads[name] = pltpu.make_async_copy(source, to, load.at[at])
        loads[name].start()

    gx, gy = lax.axis_index("gx"), lax.axis_index("gy")
    place = {"x": gx % 4, "z": gx // 4 % 4, "y": gx // 16 * 2 + gy // 2}
    core = gy % 2

    def device(**moves):
        spot = {**place, **moves}
        return {"gx": spot["y"] // 2 * 16 + spot["z"] * 4 + spot["x"], "gy": spot["y"] % 2 * 2 + core}

    sibling = {"gx": gx, "gy": gy - core + 1 - core}

    def remote(src, dst, send_sem, recv_sem, peer):
        return pltpu.make_async_remote_copy(src_ref=src, dst_ref=dst, send_sem=send_sem, recv_sem=recv_sem,
                                            device_id=peer, device_id_type=MESH)

    def plane_peer(part, to):
        return device(**{ORDERS[part][1]: to // 4, ORDERS[part][2]: to % 4})

    halo2, halo1, halou, haloc = (
        Halo(buf, halo_send.at[at], halo_recv.at[at], counts) for at, buf in enumerate((d2, d1, ub, cb)))
    barrier = pltpu.get_barrier_semaphore()
    peers = [sibling] + [device(**{axis: (place[axis] + j) % 4}) for axis in "xyz" for j in (1, 2, 3)]
    for one, two in ("xy", "yz", "zx"):
        peers += [device(**{one: (place[one] + j) % 4, two: (place[two] + k) % 4})
                  for j in (1, 2, 3) for k in (1, 2, 3)]
    for peer in peers:
        pl.semaphore_signal(barrier, inc=1, device_id=peer, device_id_type=MESH)
    friends = len(peers)
    for dx, dy in SIDES:
        near = halo2.there(dx, dy)
        friends = friends + near.astype(jnp.int32)

        @pl.when(near)
        def _():
            pl.semaphore_signal(barrier, inc=1, device_id={"gx": gx + dx, "gy": gy + dy}, device_id_type=MESH)
    for halo in (halo2, halo1, halou, haloc):
        halo.clear()
    from_z = lax.broadcasted_iota(jnp.int32, sort.shape, 0)
    to_z = lax.broadcasted_iota(jnp.int32, sort.shape, 1)
    sort[...] = jnp.where(from_z == to_z % 128 * 2 + to_z // 128, 1.0, 0.0).astype(BF16)

    def sorted_plane(cells):
        by_row = jnp.swapaxes(cells, 0, 1)
        return nn(by_row.reshape(256, 256), sort[...]).astype(BF16).reshape(by_row.shape)

    loads["g"].wait()
    loads["h_two"].wait()
    for x in range(2):
        masked = jnp.where(h_two_ref[:, x].astype(F32) > 0, g_ref[:, x].astype(F32), 0.0).astype(BF16)
        d2[x + 1, 1:5] = sorted_plane(masked)
    pl.semaphore_wait(barrier, friends)
    halo2.start()

    loads["c"].wait()
    cb[1, 1:3] = jnp.swapaxes(c_ref[:, 0], 0, 1)
    loads["w2"].wait()
    conv_matrix(w2_ref, rows, a2)
    for name, source, taps, places in (("h", h_ref, h3, (0, 64, 128, 192)), ("up", up_ref, up3, (0, 64, 192, 128))):
        loads[name].wait()
        for x in range(2):
            plane = sorted_plane(source[:, x])
            for y in range(4):
                cells = plane[y]
                wide = cells.astype(F32)
                taps[x, y, places[0] : places[0] + 64] = before(wide).astype(BF16)
                taps[x, y, places[1] : places[1] + 64] = cells
                taps[x, y, places[2] : places[2] + 64] = after(wide).astype(BF16)
                taps[x, y, places[3] : places[3] + 64] = jnp.zeros_like(cells)

    halo2.wait_recv()
    haloc.start()
    for x in range(2):
        for y in range(4):
            grad = input_rows(a2[...], d2, x, y)
            d1[x + 1, y + 1] = jnp.where(h3[x, y, 64:128].astype(F32) > 0, grad, 0.0).astype(BF16)
        halo1.start((-1,) if x == 0 else (0, 1))

    loads["w1"].wait()
    conv_matrix(w1_ref, rows, a1)
    total2 = filter_grad(d2, h3)
    pack[0, :CONV_ROWS] = total2[:, :128]
    pack[0, CONV_ROWS : CONV_ROWS + MIXED_ROWS] = total2[:MIXED_ROWS, 128:]
    pack[1, CONV_ROWS : CONV_ROWS + MIXED_ROWS] = total2[MIXED_ROWS:, 128:]
    for half in range(2):
        pack[half, CONV_ROWS + MIXED_ROWS :] = jnp.zeros((PART - CONV_ROWS - MIXED_ROWS, 128), F32)
    haloc.wait_recv()
    for x in range(3):
        for y in range(4):
            cells = cb[x, y]
            wide = cells.astype(F32)
            c3[0, x, y] = moved(wide, -1).astype(BF16)
            c3[1, x, y] = cells
            c3[2, x, y] = moved(wide, 1).astype(BF16)

    halo1.wait_recv()
    for x in range(2):
        for y in range(4):
            ub[x + 1, y + 1] = input_rows(a1[...], d1, x, y).astype(BF16)
        halou.start((-1,) if x == 0 else (0, 1))

    total1 = filter_grad(d1, up3)
    pack[1, :CONV_ROWS] = total1[:, :128]
    pack[0, CONV_ROWS : CONV_ROWS + MIXED_ROWS] += total1[:MIXED_ROWS, 128:]
    pack[1, CONV_ROWS : CONV_ROWS + MIXED_ROWS] += total1[MIXED_ROWS:, 128:]
    away_mixed[...] = pack[1 - core].astype(BF16)
    mixed = remote(away_mixed, got0_mixed, core_send.at[4], core_recv.at[4], sibling)
    mixed.start()

    classes = [(py, pz) for py in range(2) for pz in range(2)]
    swaps = []
    for at, (py, pz) in enumerate(classes):
        result = class_grad(ub, c3, 1 - core, py, pz).astype(BF16)
        for n in range(8):
            away[at, n * 64 : n * 64 + 64] = result[:, n * 128 : n * 128 + 128]
        swaps.append(remote(away.at[at], got0.at[at], core_send.at[at], core_recv.at[at], sibling))
        swaps[-1].start()

    def rows_at(start, size):
        return pl.ds(pl.multiple_of(start, 16), size)

    def ring_start(part):
        axis = ORDERS[part][0]
        copies = []
        for j in (1, 2, 3):
            to = (place[axis] + j) % 4
            copies.append(remote(held.at[rows_at(part * PART + to * QUARTER, QUARTER)], got1.at[part, j - 1],
                                 ring_send.at[0, part, j - 1], ring_recv.at[0, part, j - 1], device(**{axis: to})))
            copies[-1].start()
        return copies

    rings = [None] * 3
    mixed.wait_recv()
    held[2 * PART :] = (pack[core] + got0_mixed[...].astype(F32)).astype(BF16)
    rings[2] = ring_start(2)
    for at, (py, pz) in enumerate(classes):
        result = class_grad(ub, c3, core, py, pz)
        swaps[at].wait_recv()
        for n in range(8):
            to = at * CLASS_ROWS + n * 64
            held[to : to + 64] = (
                result[:, n * 128 : n * 128 + 128] + got0[at, n * 64 : n * 64 + 64].astype(F32)).astype(BF16)
        if at % 2 == 1:
            rings[at // 2] = ring_start(at // 2)

    halou.wait_recv()
    input_grad(ub, wt_ref, loads["wt"], ig_ref)
    home = [place[ORDERS[part][0]] for part in range(3)]
    seat = [place[ORDERS[part][1]] * 4 + place[ORDERS[part][2]] for part in range(3)]
    start = [core * HALF + part * PART + home[part] * QUARTER for part in range(3)]
    planes = [None] * 3
    for part in (2, 0, 1):
        for copy in rings[part]:
            copy.wait_recv()
        total = held[rows_at(part * PART + home[part] * QUARTER, QUARTER)].astype(F32)
        for j in range(3):
            total = total + got1[part, j].astype(F32)
        own1[part] = total.astype(BF16)
        planes[part] = []
        for j in range(1, 16):
            to = (seat[part] + j) % 16
            planes[part].append(remote(own1.at[part, rows_at(to * PIECE, PIECE)], got2.at[part, j - 1],
                                       plane_send.at[0, part, j - 1], plane_recv.at[0, part, j - 1],
                                       plane_peer(part, to)))
            planes[part][-1].start()
    sent = rings[0] + rings[1] + rings[2] + planes[0] + planes[1] + planes[2] + swaps + [mixed]

    spread = [None] * 3
    for part in (2, 0, 1):
        for copy in planes[part]:
            copy.wait_recv()
        total = own1[part, rows_at(seat[part] * PIECE, PIECE)].astype(F32)
        for j in range(15):
            total = total + got2[part, j].astype(F32)
        block = out_ref.at[rows_at(start[part] + seat[part] * PIECE, PIECE)]
        out_ref[rows_at(start[part] + seat[part] * PIECE, PIECE)] = total.astype(BF16)
        spread[part] = []
        for j in range(1, 16):
            to = (seat[part] + j) % 16
            spread[part].append(remote(block, block, plane_send.at[1, part, j - 1], plane_recv.at[1, part, j - 1],
                                       plane_peer(part, to)))
            spread[part][-1].start()
    shares = []

    def share(at, from_row):
        block = out_ref.at[rows_at(from_row, QUARTER)]
        shares.append(remote(block, block, core_send.at[5 + at], core_recv.at[5 + at], sibling))
        shares[-1].start()

    back = [None] * 3
    for part in (2, 0, 1):
        axis = ORDERS[part][0]
        for copy in spread[part]:
            copy.wait_recv()
        block = out_ref.at[rows_at(start[part], QUARTER)]
        back[part] = []
        for j in (1, 2, 3):
            back[part].append(remote(block, block, ring_send.at[1, part, j - 1], ring_recv.at[1, part, j - 1],
                                     device(**{axis: (place[axis] + j) % 4})))
            back[part][-1].start()
        share(part, start[part])
    for j in (1, 3, 2):
        for part in (2, 0, 1):
            back[part][j - 1].wait_recv()
            share(j * 3 + part, core * HALF + part * PART + (home[part] + 4 - j) % 4 * QUARTER)
    for copy in shares:
        copy.wait_recv()
    sent += spread[0] + spread[1] + spread[2] + back[0] + back[1] + back[2] + shares
    for copy in sent:
        copy.wait_send()
    for halo in (halo2, halo1, halou, haloc):
        halo.wait_send()


def input_grad(ub, wt_ref, load, ig_ref):
    load.wait()
    sums = []
    for half in range(2):
        around = jnp.concatenate(
            [ub[:, 2 * row : 2 * row + 4, :, half * 128 : half * 128 + 128].reshape(1024, 128) for row in range(2)],
            axis=1)
        filters = jnp.concatenate(
            [jnp.concatenate([wt_ref[4 * at + kz] for at in range(16)], axis=0) for kz in (1 - half, 3 - half)], axis=1)
        sums.append(lax.dot_general(filters, around, (((0,), (0,)), ((), ())), preferred_element_type=F32))
    even, odd = sums
    for row in range(2):
        lanes = slice(row * 128, row * 128 + 128)
        ig_ref[row] = (even[:128, lanes] + moved(even[128:, lanes], 1)
                       + odd[128:, lanes] + moved(odd[:128, lanes], -1)).astype(BF16)


def widen(scale, rows_ref, ig_rows_ref, ig_any, tconv_any, one_any, two_any, ig_ref, tconv_ref, one_ref, two_ref, done):
    writes = []

    def write(source, to):
        writes.append(pltpu.make_async_copy(source, to, done.at[len(writes)]))
        writes[-1].start()

    row_of = {}
    for px in range(2):
        for at in range(4):
            n = 0
            for kx, _ in tap_choices(px):
                for ky, _ in tap_choices(at // 2):
                    for kz, _ in tap_choices(at % 2):
                        row_of[16 * kx + 4 * ky + kz] = px * HALF + at * CLASS_ROWS + n * 64
                        n += 1
    for chunk in range(8):
        for tap in range(8 * chunk, 8 * chunk + 8):
            tconv_ref[tap] = rows_ref[row_of[tap] : row_of[tap] + 64].astype(F32) * scale
        write(tconv_ref.at[pl.ds(8 * chunk, 8)], tconv_any.at[pl.ds(8 * chunk, 8)])

    def mixed(start, size):
        half, inside = start // MIXED_ROWS, start % MIXED_ROWS
        at = half * HALF + 2 * PART + CONV_ROWS + inside
        many = min(size, MIXED_ROWS - inside)
        found = rows_ref[at : at + many].astype(F32)
        return found if many == size else jnp.concatenate([found, mixed(start + many, size - many)], axis=0)

    for a in range(3):
        for b in range(3):
            at = ((2 - a) * 3 + 2 - b) * 64
            low2 = rows_ref[2 * PART + at : 2 * PART + at + 64].astype(F32) * scale
            low1 = rows_ref[HALF + 2 * PART + at : HALF + 2 * PART + at + 64].astype(F32) * scale
            high = mixed(at, 64) * scale
            tap = 9 * a + 3 * b
            two_ref[tap] = low2[:, :64]
            two_ref[tap + 1] = low2[:, 64:]
            two_ref[tap + 2] = high[:, :64]
            one_ref[tap] = low1[:, :64]
            one_ref[tap + 1] = low1[:, 64:]
            one_ref[tap + 2] = high[:, 64:]
        write(two_ref.at[pl.ds(9 * a, 9)], two_any.at[pl.ds(9 * a, 9)])
        write(one_ref.at[pl.ds(9 * a, 9)], one_any.at[pl.ds(9 * a, 9)])
    ig_ref[:, 0] = jnp.swapaxes(ig_rows_ref[...], 0, 1)
    write(ig_ref, ig_any)
    for copy in writes:
        copy.wait()


def shards(counts, coarse_input, upsampled, hidden_one, hidden_two, cotangent,
           tconv_weight, conv_one_weight, conv_two_weight):
    channels, planes, across, length = cotangent.shape
    scale = 1.0 / math.sqrt(planes * counts[0] * across * counts[1] * length)
    vmem, anywhere = pl.BlockSpec(memory_space=pltpu.VMEM), pl.BlockSpec(memory_space=pl.ANY)
    args = (coarse_input, upsampled, hidden_one, hidden_two, cotangent, tconv_weight, conv_one_weight, conv_two_weight)
    haloed = pltpu.VMEM((4, 6, channels, length), BF16)
    shifted = pltpu.VMEM((2, 4, 256, length), BF16)
    dma = pltpu.SemaphoreType.DMA
    input_rows, total = pl.pallas_call(
        functools.partial(section, counts),
        out_shape=(jax.ShapeDtypeStruct((2, 128, 128), BF16), jax.ShapeDtypeStruct((ROWS, 128), BF16)),
        in_specs=[pl.BlockSpec(memory_space=pltpu.HBM)] * 8,
        out_specs=(vmem, vmem),
        scratch_shapes=[pltpu.VMEM(arg.shape, arg.dtype) for arg in args] + [
            haloed, haloed, haloed, pltpu.VMEM((3, 4, 128, 128), BF16),
            shifted, shifted, pltpu.VMEM((3, 3, 4, 128, 128), BF16),
            pltpu.VMEM((CONV_ROWS, 256), BF16), pltpu.VMEM((192, CONV_ROWS), BF16), pltpu.VMEM((192, CONV_ROWS), BF16),
            pltpu.VMEM((length, length), BF16), pltpu.VMEM((2, PART, 128), F32),
            pltpu.VMEM((4, CLASS_ROWS, 128), BF16), pltpu.VMEM((PART, 128), BF16),
            pltpu.VMEM((4, CLASS_ROWS, 128), BF16), pltpu.VMEM((PART, 128), BF16),
            pltpu.VMEM((HALF, 128), BF16),
            pltpu.VMEM((3, 3, QUARTER, 128), BF16),
            pltpu.VMEM((3, 15, PIECE, 128), BF16),
            pltpu.VMEM((3, QUARTER, 128), BF16),
            dma((8,)), dma((4, 8)), dma((4, 8)), dma((17,)), dma((17,)),
            dma((2, 3, 3)), dma((2, 3, 3)), dma((2, 3, 15)), dma((2, 3, 15)),
        ],
        compiler_params=pltpu.CompilerParams(collective_id=0, has_side_effects=True, vmem_limit_bytes=VMEM_BYTES),
    )(*args)

    shapes = (((128, 1, 2, 128), BF16), ((64, 64, 128), F32), ((27, 64, 64), F32), ((27, 64, 64), F32))
    return pl.pallas_call(
        functools.partial(widen, scale),
        out_shape=tuple(jax.ShapeDtypeStruct(*shape) for shape in shapes),
        in_specs=[vmem, vmem],
        out_specs=(anywhere,) * 4,
        scratch_shapes=[pltpu.VMEM(*shape) for shape in shapes] + [dma((15,))],
        compiler_params=pltpu.CompilerParams(vmem_limit_bytes=VMEM_BYTES),
    )(total, input_rows)


def solution(mesh):
    cells = P(None, "gx", "gy", None)
    return jax.shard_map(
        functools.partial(shards, (mesh.shape["gx"], mesh.shape["gy"])),
        mesh=mesh,
        in_specs=(cells,) * 5 + (P(),) * 3,
        out_specs=(cells, P(), P(), P()),
        check_vma=False,
    )
```

```python
import functools
import math

import jax
import jax.numpy as jnp
from jax import lax
from jax.experimental import pallas as pl
from jax.experimental.pallas import tpu as pltpu
from jax.sharding import PartitionSpec as P

BF16 = jnp.bfloat16
F32 = jnp.float32
MESH = pl.DeviceIdType.MESH
SIDES = [(dx, dy) for dx in (-1, 0, 1) for dy in (-1, 0, 1) if dx or dy]
VMEM_BYTES = 56 * 1024 * 1024

CONV_ROWS = 576
MIXED_ROWS = CONV_ROWS // 2
PART = 1024
HALF = 3 * PART
ROWS = 2 * HALF
QUARTER = PART // 4
PIECE = QUARTER // 16
ORDERS = ("xyz", "yzx", "zxy")


def nn(a, b):
    return lax.dot_general(a, b, (((1,), (0,)), ((), ())), preferred_element_type=F32)


def nt(a, b):
    return lax.dot_general(a, b, (((1,), (1,)), ((), ())), preferred_element_type=F32)


def moved(cells, by):
    length = cells.shape[-1]
    lane = lax.broadcasted_iota(jnp.int32, cells.shape, cells.ndim - 1)
    rolled = pltpu.roll(cells, (-by) % length, cells.ndim - 1)
    return jnp.where(lane == (0 if by < 0 else length - 1), 0.0, rolled)


def exists(gx, gy, dx, dy, count_x, count_y):
    found = []
    if dx < 0:
        found.append(gx > 0)
    if dx > 0:
        found.append(gx < count_x - 1)
    if dy < 0:
        found.append(gy > 0)
    if dy > 0:
        found.append(gy < count_y - 1)
    return functools.reduce(jnp.logical_and, found)


class Halo:
    def __init__(self, buf, send, recv, counts):
        self.buf, self.send, self.recv, self.counts = buf, send, recv, counts
        self.planes, self.rows = buf.shape[0] - 2, buf.shape[1] - 2
        self.gx, self.gy = lax.axis_index("gx"), lax.axis_index("gy")

    def clear(self):
        ends = ((self.gx == 0, 0, None), (self.gx == self.counts[0] - 1, self.planes + 1, None),
                (self.gy == 0, None, 0), (self.gy == self.counts[1] - 1, None, self.rows + 1))
        for at_end, plane, row in ends:
            @pl.when(at_end)
            def _():
                if plane is not None:
                    self.buf[plane] = jnp.zeros(self.buf.shape[1:], BF16)
                else:
                    self.buf[:, row] = jnp.zeros(self.buf.shape[:1] + self.buf.shape[2:], BF16)

    def copy(self, k):
        dx, dy = SIDES[k]

        def cut(step, size):
            if step == 0:
                return (1, 1, size)
            return (1, size + 1, 1) if step < 0 else (size, 0, 1)

        from_x, to_x, many_x = cut(dx, self.planes)
        from_y, to_y, many_y = cut(dy, self.rows)
        return pltpu.make_async_remote_copy(
            src_ref=self.buf.at[pl.ds(from_x, many_x), pl.ds(from_y, many_y)],
            dst_ref=self.buf.at[pl.ds(to_x, many_x), pl.ds(to_y, many_y)],
            send_sem=self.send.at[k],
            recv_sem=self.recv.at[k],
            device_id={"gx": self.gx + dx, "gy": self.gy + dy},
            device_id_type=MESH,
        )

    def there(self, dx, dy):
        return exists(self.gx, self.gy, dx, dy, *self.counts)

    def start(self, steps=(-1, 0, 1)):
        for k, (dx, dy) in enumerate(SIDES):
            if dx not in steps:
                continue

            @pl.when(self.there(dx, dy))
            def _():
                self.copy(k).start()

    def wait_recv(self, steps=(-1, 0, 1)):
        for k, (dx, dy) in enumerate(SIDES):
            if dx not in steps:
                continue

            @pl.when(self.there(-dx, -dy))
            def _():
                self.copy(k).wait_recv()

    def wait_send(self):
        for k, (dx, dy) in enumerate(SIDES):
            @pl.when(self.there(dx, dy))
            def _():
                self.copy(k).wait_send()


def before(cells):
    half = cells.shape[-1] // 2
    return jnp.concatenate([moved(cells[..., half:], -1), cells[..., :half]], axis=-1)


def after(cells):
    half = cells.shape[-1] // 2
    return jnp.concatenate([cells[..., half:], moved(cells[..., :half], 1)], axis=-1)


def input_rows(weights, halo_ref, x, y):
    window = halo_ref[pl.ds(x, 3), y : y + 3].reshape(weights.shape[1], halo_ref.shape[3])
    taps = nn(weights, window)
    size = taps.shape[0] // 3
    return after(taps[:size]) + taps[size : 2 * size] + before(taps[2 * size :])


def filter_grad(halo_ref, taps_ref):
    rows = [(x, y) for x in range(2) for y in range(4)]
    windows = [halo_ref[x : x + 3, y : y + 3].reshape(CONV_ROWS, halo_ref.shape[3]) for x, y in rows]
    return nt(jnp.concatenate(windows, axis=1), jnp.concatenate([taps_ref[x, y] for x, y in rows], axis=1))


def conv_matrix(weight_ref, rows_ref, matrix_ref):
    rows_ref[:, 192:] = jnp.zeros((CONV_ROWS, 64), BF16)
    for a in range(3):
        for b in range(3):
            at = ((2 - a) * 3 + 2 - b) * 64
            for c in range(3):
                rows_ref[at : at + 64, c * 64 : c * 64 + 64] = weight_ref[9 * a + 3 * b + c]
    matrix_ref[...] = rows_ref[...].T[:192]


def tap_choices(parity):
    return ((2, 1), (0, 2)) if parity else ((1, 1), (3, 0))


def class_grad(fine, coarse, py, pz):
    own = jnp.concatenate(
        [cells(2 * row + py)[:, pz * 128 : pz * 128 + 128] for cells in fine for row in range(2)], axis=1)
    parts = []
    for nx in range(2):
        for _, sy in tap_choices(py):
            for _, sz in tap_choices(pz):
                parts.append(jnp.concatenate([c3[sz, nx, row + sy] for c3 in coarse for row in range(2)], axis=1))
    return nt(own, jnp.concatenate(parts, axis=0))


def section(counts, c_any, up_any, h_any, h_two_any, g_any, wt_any, w1_any, w2_any, ig_ref, out_ref,
            c_ref, up_ref, h_ref, h_two_ref, g_ref, wt_ref, w1_ref, w2_ref,
            d2, d1, ub, cb, us, cs, h3, up3, c3, c3s, rows, a2, a1, sort, total2, total1, away, got0,
            held, got1, got2, own1,
            load, halo_send, halo_recv, core_send, core_recv, ring_send, ring_recv, plane_send, plane_recv):
    loads = {}
    for at, (name, source, to) in enumerate((
            ("g", g_any, g_ref), ("h_two", h_two_any, h_two_ref), ("c", c_any, c_ref), ("w2", w2_any, w2_ref),
            ("h", h_any, h_ref), ("up", up_any, up_ref), ("w1", w1_any, w1_ref), ("wt", wt_any, wt_ref))):
        loads[name] = pltpu.make_async_copy(source, to, load.at[at])
        loads[name].start()

    gx, gy = lax.axis_index("gx"), lax.axis_index("gy")
    place = {"x": gx % 4, "z": gx // 4 % 4, "y": gx // 16 * 2 + gy // 2}
    core = gy % 2

    def device(**moves):
        spot = {**place, **moves}
        return {"gx": spot["y"] // 2 * 16 + spot["z"] * 4 + spot["x"], "gy": spot["y"] % 2 * 2 + core}

    sibling = {"gx": gx, "gy": gy - core + 1 - core}

    def remote(src, dst, send_sem, recv_sem, peer):
        return pltpu.make_async_remote_copy(src_ref=src, dst_ref=dst, send_sem=send_sem, recv_sem=recv_sem,
                                            device_id=peer, device_id_type=MESH)

    def rows_at(start, size):
        return pl.ds(pl.multiple_of(start, 16), size)

    def plane_peer(part, to):
        return device(**{ORDERS[part][1]: to // 4, ORDERS[part][2]: to % 4})

    halo2, halo1, halou, haloc = (
        Halo(buf, halo_send.at[at], halo_recv.at[at], counts) for at, buf in enumerate((d2, d1, ub, cb)))
    barrier = pltpu.get_barrier_semaphore()
    peers = [sibling] + [device(**{axis: (place[axis] + j) % 4}) for axis in "xyz" for j in (1, 2, 3)]
    for one, two in ("xy", "yz", "zx"):
        peers += [device(**{one: (place[one] + j) % 4, two: (place[two] + k) % 4})
                  for j in (1, 2, 3) for k in (1, 2, 3)]
    for peer in peers:
        pl.semaphore_signal(barrier, inc=1, device_id=peer, device_id_type=MESH)
    friends = len(peers)
    for dx, dy in SIDES:
        near = halo2.there(dx, dy)
        friends = friends + near.astype(jnp.int32)

        @pl.when(near)
        def _():
            pl.semaphore_signal(barrier, inc=1, device_id={"gx": gx + dx, "gy": gy + dy}, device_id_type=MESH)
    from_z = lax.broadcasted_iota(jnp.int32, sort.shape, 0)
    to_z = lax.broadcasted_iota(jnp.int32, sort.shape, 1)
    sort[...] = jnp.where(from_z == to_z % 128 * 2 + to_z // 128, 1.0, 0.0).astype(BF16)

    def sorted_plane(cells):
        by_row = jnp.swapaxes(cells, 0, 1)
        return nn(by_row.reshape(256, 256), sort[...]).astype(BF16).reshape(by_row.shape)

    loads["g"].wait()
    loads["h_two"].wait()
    for x in range(2):
        masked = jnp.where(h_two_ref[:, x].astype(F32) > 0, g_ref[:, x].astype(F32), 0.0).astype(BF16)
        d2[x + 1, 1:5] = sorted_plane(masked)
    pl.semaphore_wait(barrier, friends)
    halo2.start()
    for halo in (halo2, halo1, halou, haloc):
        halo.clear()

    loads["c"].wait()
    cb[1, 1:3] = jnp.swapaxes(c_ref[:, 0], 0, 1)
    loads["w2"].wait()
    conv_matrix(w2_ref, rows, a2)
    for name, source, taps, places in (("h", h_ref, h3, (0, 64, 128, 192)), ("up", up_ref, up3, (0, 64, 192, 128))):
        loads[name].wait()
        for x in range(2):
            plane = sorted_plane(source[:, x])
            for y in range(4):
                cells = plane[y]
                wide = cells.astype(F32)
                taps[x, y, places[0] : places[0] + 64] = before(wide).astype(BF16)
                taps[x, y, places[1] : places[1] + 64] = cells
                taps[x, y, places[2] : places[2] + 64] = after(wide).astype(BF16)
                taps[x, y, places[3] : places[3] + 64] = jnp.zeros_like(cells)

    halo2.wait_send()
    haloc.start()

    for x in range(2):
        halo2.wait_recv((0, 1) if x == 0 else (-1,))
        for y in range(4):
            grad = input_rows(a2[...], d2, x, y)
            d1[x + 1, y + 1] = jnp.where(h3[x, y, 64:128].astype(F32) > 0, grad, 0.0).astype(BF16)
        halo1.start((-1,) if x == 0 else (0, 1))

    loads["w1"].wait()
    conv_matrix(w1_ref, rows, a1)
    total2[...] = filter_grad(d2, h3)
    away[0] = total2[rows_at((1 - core) * MIXED_ROWS, MIXED_ROWS)].astype(BF16)
    swaps = [remote(away.at[0], got0.at[0], core_send.at[0], core_recv.at[0], sibling)]
    swaps[0].start()
    haloc.wait_recv()
    swaps.append(remote(cb, cs, core_send.at[1], core_recv.at[1], sibling))
    swaps[1].start()

    def shift_coarse(cells_ref, to_ref):
        for nx, x in enumerate((1, 2 * core)):
            for y in range(4):
                cells = cells_ref[x, y]
                wide = cells.astype(F32)
                to_ref[0, nx, y] = moved(wide, -1).astype(BF16)
                to_ref[1, nx, y] = cells
                to_ref[2, nx, y] = moved(wide, 1).astype(BF16)

    shift_coarse(cb, c3)
    swaps[1].wait_recv()
    shift_coarse(cs, c3s)

    halo1.wait_recv()
    for x in (1 - core, core):
        for y in range(4):
            ub[x + 1, y + 1] = input_rows(a1[...], d1, x, y).astype(BF16)
        if len(swaps) == 2:
            swaps.append(remote(ub.at[x + 1, pl.ds(1, 4)], us, core_send.at[2], core_recv.at[2], sibling))
            swaps[2].start()
    total1[...] = filter_grad(d1, up3)
    away[1] = total1[rows_at((1 - core) * MIXED_ROWS, MIXED_ROWS)].astype(BF16)
    swaps.append(remote(away.at[1], got0.at[1], core_send.at[3], core_recv.at[3], sibling))
    swaps[3].start()

    def ring_start(part):
        axis = ORDERS[part][0]
        copies = []
        for j in (1, 2, 3):
            to = (place[axis] + j) % 4
            copies.append(remote(held.at[rows_at(part * PART + to * QUARTER, QUARTER)], got1.at[part, j - 1],
                                 ring_send.at[0, part, j - 1], ring_recv.at[0, part, j - 1], device(**{axis: to})))
            copies[-1].start()
        return copies

    swaps[2].wait_recv()
    fine = (lambda row: ub[1 + core, 1 + row], lambda row: us[row])
    for py in range(2):
        for pz in range(2):
            result = class_grad(fine, (c3, c3s), py, pz).astype(BF16)
            n = 0
            for nx in range(2):
                for ky, _ in tap_choices(py):
                    for kz, _ in tap_choices(pz):
                        to = nx * PART + (4 * ky + kz) * 64
                        held[to : to + 64] = result[:, n * 128 : n * 128 + 128]
                        n += 1
    rings = [ring_start(0), ring_start(1)]
    swaps[0].wait_recv()
    swaps[3].wait_recv()
    mine = rows_at(core * MIXED_ROWS, MIXED_ROWS)
    sum2 = total2[mine] + got0[0].astype(F32)
    sum1 = total1[mine] + got0[1].astype(F32)
    for at, rows_of in enumerate((sum2[:, :128], sum1[:, :128], sum2[:, 128:] + sum1[:, 128:])):
        to = 2 * PART + at * MIXED_ROWS
        held[to : to + MIXED_ROWS] = rows_of.astype(BF16)
    held[2 * PART + 3 * MIXED_ROWS :] = jnp.zeros((PART - 3 * MIXED_ROWS, 128), BF16)
    rings.append(ring_start(2))

    home = [place[ORDERS[part][0]] for part in range(3)]
    seat = [place[ORDERS[part][1]] * 4 + place[ORDERS[part][2]] for part in range(3)]
    start = [core * HALF + part * PART + home[part] * QUARTER for part in range(3)]
    planes = [None] * 3
    for part in (0, 1, 2):
        for copy in rings[part]:
            copy.wait_recv()
        total = held[rows_at(part * PART + home[part] * QUARTER, QUARTER)].astype(F32)
        for j in range(3):
            total = total + got1[part, j].astype(F32)
        own1[part] = total.astype(BF16)
        planes[part] = []
        for j in range(1, 16):
            to = (seat[part] + j) % 16
            planes[part].append(remote(own1.at[part, rows_at(to * PIECE, PIECE)], got2.at[part, j - 1],
                                       plane_send.at[0, part, j - 1], plane_recv.at[0, part, j - 1],
                                       plane_peer(part, to)))
            planes[part][-1].start()
    halou.start()
    sent = rings[0] + rings[1] + rings[2] + planes[0] + planes[1] + planes[2] + swaps

    spread = [None] * 3
    for part in (0, 1, 2):
        for copy in planes[part]:
            copy.wait_recv()
        total = own1[part, rows_at(seat[part] * PIECE, PIECE)].astype(F32)
        for j in range(15):
            total = total + got2[part, j].astype(F32)
        block = out_ref.at[rows_at(start[part] + seat[part] * PIECE, PIECE)]
        out_ref[rows_at(start[part] + seat[part] * PIECE, PIECE)] = total.astype(BF16)
        spread[part] = []
        for j in range(1, 16):
            to = (seat[part] + j) % 16
            spread[part].append(remote(block, block, plane_send.at[1, part, j - 1], plane_recv.at[1, part, j - 1],
                                       plane_peer(part, to)))
            spread[part][-1].start()
    halou.wait_recv()
    input_grad(ub, wt_ref, loads["wt"], ig_ref)
    shares = []

    def share(at, from_row):
        block = out_ref.at[rows_at(from_row, QUARTER)]
        shares.append(remote(block, block, core_send.at[5 + at], core_recv.at[5 + at], sibling))
        shares[-1].start()

    back = [None] * 3
    for part in (0, 1, 2):
        axis = ORDERS[part][0]
        for copy in spread[part]:
            copy.wait_recv()
        block = out_ref.at[rows_at(start[part], QUARTER)]
        back[part] = []
        for j in (1, 2, 3):
            back[part].append(remote(block, block, ring_send.at[1, part, j - 1], ring_recv.at[1, part, j - 1],
                                     device(**{axis: (place[axis] + j) % 4})))
            back[part][-1].start()
        share(part, start[part])
    for j in (1, 3, 2):
        for part in (0, 1, 2):
            back[part][j - 1].wait_recv()
            share(j * 3 + part, core * HALF + part * PART + (home[part] + 4 - j) % 4 * QUARTER)
    for copy in shares:
        copy.wait_recv()
    sent += spread[0] + spread[1] + spread[2] + back[0] + back[1] + back[2] + shares
    for copy in sent:
        copy.wait_send()
    for halo in (halo1, halou, haloc):
        halo.wait_send()


def input_grad(ub, wt_ref, load, ig_ref):
    load.wait()
    sums = []
    for half in range(2):
        around = jnp.concatenate(
            [ub[:, 2 * row : 2 * row + 4, :, half * 128 : half * 128 + 128].reshape(1024, 128) for row in range(2)],
            axis=1)
        filters = jnp.concatenate(
            [jnp.concatenate([wt_ref[4 * at + kz] for at in range(16)], axis=0) for kz in (1 - half, 3 - half)], axis=1)
        sums.append(lax.dot_general(filters, around, (((0,), (0,)), ((), ())), preferred_element_type=F32))
    even, odd = sums
    for row in range(2):
        lanes = slice(row * 128, row * 128 + 128)
        ig_ref[row] = (even[:128, lanes] + moved(even[128:, lanes], 1)
                       + odd[128:, lanes] + moved(odd[:128, lanes], -1)).astype(BF16)


def widen(scale, rows_any, ig_rows_any, ig_any, tconv_any, one_any, two_any,
          rows_ref, ig_rows_ref, ig_ref, tconv_ref, one_ref, two_ref, load, done):
    spans = [half * HALF + part * PART for part in range(3) for half in range(2)]
    reads = [pltpu.make_async_copy(rows_any.at[pl.ds(start, PART)], rows_ref.at[pl.ds(start, PART)], load.at[at])
             for at, start in enumerate(spans)]
    reads.append(pltpu.make_async_copy(ig_rows_any, ig_rows_ref, load.at[len(spans)]))
    for copy in reads:
        copy.start()
    writes = []

    def write(source, to):
        writes.append(pltpu.make_async_copy(source, to, done.at[len(writes)]))
        writes[-1].start()

    for at, kx in enumerate((1, 2, 3, 0)):
        reads[at].wait()
        cells = rows_ref[spans[at] : spans[at] + PART].astype(F32) * scale
        tconv_ref[16 * kx : 16 * kx + 16] = cells.reshape(16, 64, 128)
        write(tconv_ref.at[pl.ds(16 * kx, 16)], tconv_any.at[pl.ds(16 * kx, 16)])
    for copy in reads[4:]:
        copy.wait()

    def piece(kind, start, size):
        half, inside = start // MIXED_ROWS, start % MIXED_ROWS
        at = half * HALF + 2 * PART + kind * MIXED_ROWS + inside
        many = min(size, MIXED_ROWS - inside)
        found = rows_ref[at : at + many].astype(F32) * scale
        return found if many == size else jnp.concatenate([found, piece(kind, start + many, size - many)], axis=0)

    for a in range(3):
        for b in range(3):
            low2, low1, high = (piece(kind, ((2 - a) * 3 + 2 - b) * 64, 64) for kind in range(3))
            tap = 9 * a + 3 * b
            two_ref[tap] = low2[:, :64]
            two_ref[tap + 1] = low2[:, 64:]
            two_ref[tap + 2] = high[:, :64]
            one_ref[tap] = low1[:, :64]
            one_ref[tap + 1] = low1[:, 64:]
            one_ref[tap + 2] = high[:, 64:]
    write(two_ref, two_any)
    write(one_ref, one_any)
    ig_ref[:, 0] = jnp.swapaxes(ig_rows_ref[...], 0, 1)
    write(ig_ref, ig_any)
    for copy in writes:
        copy.wait()


def shards(counts, coarse_input, upsampled, hidden_one, hidden_two, cotangent,
           tconv_weight, conv_one_weight, conv_two_weight):
    channels, planes, across, length = cotangent.shape
    scale = 1.0 / math.sqrt(planes * counts[0] * across * counts[1] * length)
    vmem, anywhere = pl.BlockSpec(memory_space=pltpu.VMEM), pl.BlockSpec(memory_space=pl.ANY)
    args = (coarse_input, upsampled, hidden_one, hidden_two, cotangent, tconv_weight, conv_one_weight, conv_two_weight)
    haloed = pltpu.VMEM((4, 6, channels, length), BF16)
    shifted = pltpu.VMEM((2, 4, 256, length), BF16)
    dma = pltpu.SemaphoreType.DMA
    input_rows, total = pl.pallas_call(
        functools.partial(section, counts),
        out_shape=(jax.ShapeDtypeStruct((2, 128, 128), BF16), jax.ShapeDtypeStruct((ROWS, 128), BF16)),
        in_specs=[pl.BlockSpec(memory_space=pltpu.HBM)] * 8,
        out_specs=(vmem, vmem),
        scratch_shapes=[pltpu.VMEM(arg.shape, arg.dtype) for arg in args] + [
            haloed, haloed, haloed, pltpu.VMEM((3, 4, 128, 128), BF16),
            pltpu.VMEM((4, channels, length), BF16), pltpu.VMEM((3, 4, 128, 128), BF16),
            shifted, shifted, pltpu.VMEM((3, 2, 4, 128, 128), BF16), pltpu.VMEM((3, 2, 4, 128, 128), BF16),
            pltpu.VMEM((CONV_ROWS, 256), BF16), pltpu.VMEM((192, CONV_ROWS), BF16), pltpu.VMEM((192, CONV_ROWS), BF16),
            pltpu.VMEM((length, length), BF16), pltpu.VMEM((CONV_ROWS, 256), F32), pltpu.VMEM((CONV_ROWS, 256), F32),
            pltpu.VMEM((2, MIXED_ROWS, 256), BF16), pltpu.VMEM((2, MIXED_ROWS, 256), BF16),
            pltpu.VMEM((HALF, 128), BF16),
            pltpu.VMEM((3, 3, QUARTER, 128), BF16),
            pltpu.VMEM((3, 15, PIECE, 128), BF16),
            pltpu.VMEM((3, QUARTER, 128), BF16),
            dma((8,)), dma((4, 8)), dma((4, 8)), dma((17,)), dma((17,)),
            dma((2, 3, 3)), dma((2, 3, 3)), dma((2, 3, 15)), dma((2, 3, 15)),
        ],
        compiler_params=pltpu.CompilerParams(collective_id=0, has_side_effects=True, vmem_limit_bytes=VMEM_BYTES),
    )(*args)

    shapes = (((128, 1, 2, 128), BF16), ((64, 64, 128), F32), ((27, 64, 64), F32), ((27, 64, 64), F32))
    return pl.pallas_call(
        functools.partial(widen, scale),
        out_shape=tuple(jax.ShapeDtypeStruct(*shape) for shape in shapes),
        in_specs=[anywhere, anywhere],
        out_specs=(anywhere,) * 4,
        scratch_shapes=[pltpu.VMEM((ROWS, 128), BF16), pltpu.VMEM((2, 128, 128), BF16)]
        + [pltpu.VMEM(*shape) for shape in shapes] + [dma((7,)), dma((7,))],
        compiler_params=pltpu.CompilerParams(vmem_limit_bytes=VMEM_BYTES),
    )(total, input_rows)


def solution(mesh):
    cells = P(None, "gx", "gy", None)
    return jax.shard_map(
        functools.partial(shards, (mesh.shape["gx"], mesh.shape["gy"])),
        mesh=mesh,
        in_specs=(cells,) * 5 + (P(),) * 3,
        out_specs=(cells, P(), P(), P()),
        check_vma=False,
    )
```

```python
import functools
import math

import jax
import jax.numpy as jnp
from jax import lax
from jax.experimental import pallas as pl
from jax.experimental.pallas import tpu as pltpu
from jax.sharding import PartitionSpec as P

BF16 = jnp.bfloat16
F32 = jnp.float32
MESH = pl.DeviceIdType.MESH
SIDES = [(dx, dy) for dx in (-1, 0, 1) for dy in (-1, 0, 1) if dx or dy]
VMEM_BYTES = 56 * 1024 * 1024

CONV_ROWS = 576
MIXED_ROWS = CONV_ROWS // 2
PART = 1024
HALF = 3 * PART
ROWS = 2 * HALF
QUARTER = PART // 4
PIECE = QUARTER // 16
CHUNKS = 1
CHUNK = QUARTER // CHUNKS
ORDERS = ("xyz", "yzx", "zxy")
RING = (2, 1, 3)
PLANE = sorted(((b, c) for b in range(4) for c in range(4) if b or c), key=lambda s: -min(s[0], 4 - s[0]) - min(s[1], 4 - s[1]))


def nn(a, b):
    return lax.dot_general(a, b, (((1,), (0,)), ((), ())), preferred_element_type=F32)


def nt(a, b):
    return lax.dot_general(a, b, (((1,), (1,)), ((), ())), preferred_element_type=F32)


def moved(cells, by):
    length = cells.shape[-1]
    lane = lax.broadcasted_iota(jnp.int32, cells.shape, cells.ndim - 1)
    rolled = pltpu.roll(cells, (-by) % length, cells.ndim - 1)
    return jnp.where(lane == (0 if by < 0 else length - 1), 0.0, rolled)


def exists(gx, gy, dx, dy, count_x, count_y):
    found = []
    if dx < 0:
        found.append(gx > 0)
    if dx > 0:
        found.append(gx < count_x - 1)
    if dy < 0:
        found.append(gy > 0)
    if dy > 0:
        found.append(gy < count_y - 1)
    return functools.reduce(jnp.logical_and, found)


class Halo:
    def __init__(self, buf, send, recv, counts):
        self.buf, self.send, self.recv, self.counts = buf, send, recv, counts
        self.planes, self.rows = buf.shape[0] - 2, buf.shape[1] - 2
        self.gx, self.gy = lax.axis_index("gx"), lax.axis_index("gy")

    def clear(self):
        ends = ((self.gx == 0, 0, None), (self.gx == self.counts[0] - 1, self.planes + 1, None),
                (self.gy == 0, None, 0), (self.gy == self.counts[1] - 1, None, self.rows + 1))
        for at_end, plane, row in ends:
            @pl.when(at_end)
            def _():
                if plane is not None:
                    self.buf[plane] = jnp.zeros(self.buf.shape[1:], BF16)
                else:
                    self.buf[:, row] = jnp.zeros(self.buf.shape[:1] + self.buf.shape[2:], BF16)

    def copy(self, k):
        dx, dy = SIDES[k]

        def cut(step, size):
            if step == 0:
                return (1, 1, size)
            return (1, size + 1, 1) if step < 0 else (size, 0, 1)

        from_x, to_x, many_x = cut(dx, self.planes)
        from_y, to_y, many_y = cut(dy, self.rows)
        return pltpu.make_async_remote_copy(
            src_ref=self.buf.at[pl.ds(from_x, many_x), pl.ds(from_y, many_y)],
            dst_ref=self.buf.at[pl.ds(to_x, many_x), pl.ds(to_y, many_y)],
            send_sem=self.send.at[k],
            recv_sem=self.recv.at[k],
            device_id={"gx": self.gx + dx, "gy": self.gy + dy},
            device_id_type=MESH,
        )

    def there(self, dx, dy):
        return exists(self.gx, self.gy, dx, dy, *self.counts)

    def start(self, steps=(-1, 0, 1)):
        for k, (dx, dy) in enumerate(SIDES):
            if dx not in steps:
                continue

            @pl.when(self.there(dx, dy))
            def _():
                self.copy(k).start()

    def wait_recv(self, steps=(-1, 0, 1)):
        for k, (dx, dy) in enumerate(SIDES):
            if dx not in steps:
                continue

            @pl.when(self.there(-dx, -dy))
            def _():
                self.copy(k).wait_recv()

    def wait_send(self):
        for k, (dx, dy) in enumerate(SIDES):
            @pl.when(self.there(dx, dy))
            def _():
                self.copy(k).wait_send()


def before(cells):
    half = cells.shape[-1] // 2
    return jnp.concatenate([moved(cells[..., half:], -1), cells[..., :half]], axis=-1)


def after(cells):
    half = cells.shape[-1] // 2
    return jnp.concatenate([cells[..., half:], moved(cells[..., :half], 1)], axis=-1)


def input_rows(weights, halo_ref, x, y):
    window = halo_ref[pl.ds(x, 3), y : y + 3].reshape(weights.shape[1], halo_ref.shape[3])
    taps = nn(weights, window)
    size = taps.shape[0] // 3
    return after(taps[:size]) + taps[size : 2 * size] + before(taps[2 * size :])


def filter_grad(halo_ref, taps_ref):
    rows = [(x, y) for x in range(2) for y in range(4)]
    windows = [halo_ref[x : x + 3, y : y + 3].reshape(CONV_ROWS, halo_ref.shape[3]) for x, y in rows]
    return nt(jnp.concatenate(windows, axis=1), jnp.concatenate([taps_ref[x, y] for x, y in rows], axis=1))


def conv_matrix(weight_ref, rows_ref, matrix_ref):
    rows_ref[:, 192:] = jnp.zeros((CONV_ROWS, 64), BF16)
    for a in range(3):
        for b in range(3):
            at = ((2 - a) * 3 + 2 - b) * 64
            for c in range(3):
                rows_ref[at : at + 64, c * 64 : c * 64 + 64] = weight_ref[9 * a + 3 * b + c]
    matrix_ref[...] = rows_ref[...].T[:192]


def tap_choices(parity):
    return ((2, 1), (0, 2)) if parity else ((1, 1), (3, 0))


def class_grad(fine, coarse, nx, py, pz):
    own = jnp.concatenate(
        [cells(2 * row + py)[:, pz * 128 : pz * 128 + 128] for cells in fine for row in range(2)], axis=1)
    parts = []
    for _, sy in tap_choices(py):
        for _, sz in tap_choices(pz):
            parts.append(jnp.concatenate([c3[sz, nx, row + sy] for c3 in coarse for row in range(2)], axis=1))
    return nt(own, jnp.concatenate(parts, axis=0))


def section(counts, c_any, up_any, h_any, h_two_any, g_any, wt_any, w1_any, w2_any, ig_ref, out_any,
            c_ref, up_ref, h_ref, h_two_ref, g_ref, wt_ref, w1_ref, w2_ref,
            d2, d1, ub, cb, us, cs, h3, up3, c3, c3s, rows, a2, a1, sort, total2, total1, away, got0,
            held, got1, got2, own1, out_ref,
            load, halo_send, halo_recv, core_send, core_recv, ring_send, ring_recv, plane_send, plane_recv, written):
    loads = {}
    for at, (name, source, to) in enumerate((
            ("g", g_any, g_ref), ("h_two", h_two_any, h_two_ref), ("c", c_any, c_ref), ("w2", w2_any, w2_ref),
            ("h", h_any, h_ref), ("up", up_any, up_ref), ("w1", w1_any, w1_ref), ("wt", wt_any, wt_ref))):
        loads[name] = pltpu.make_async_copy(source, to, load.at[at])
        loads[name].start()

    gx, gy = lax.axis_index("gx"), lax.axis_index("gy")
    place = {"x": gx % 4, "z": gx // 4 % 4, "y": gx // 16 * 2 + gy // 2}
    core = gy % 2

    def device(**moves):
        spot = {**place, **moves}
        return {"gx": spot["y"] // 2 * 16 + spot["z"] * 4 + spot["x"], "gy": spot["y"] % 2 * 2 + core}

    sibling = {"gx": gx, "gy": gy - core + 1 - core}

    def remote(src, dst, send_sem, recv_sem, peer):
        return pltpu.make_async_remote_copy(src_ref=src, dst_ref=dst, send_sem=send_sem, recv_sem=recv_sem,
                                            device_id=peer, device_id_type=MESH)

    def rows_at(start, size):
        return pl.ds(pl.multiple_of(start, 16), size)

    def plane_place(part, step):
        return [(place[axis] + by) % 4 for axis, by in zip(ORDERS[part][1:], step)]

    def plane_peer(part, step):
        return device(**dict(zip(ORDERS[part][1:], plane_place(part, step))))

    halo2, halo1, halou, haloc = (
        Halo(buf, halo_send.at[at], halo_recv.at[at], counts) for at, buf in enumerate((d2, d1, ub, cb)))
    barrier = pltpu.get_barrier_semaphore()
    peers = [sibling] + [device(**{axis: (place[axis] + j) % 4}) for axis in "xyz" for j in (1, 2, 3)]
    for one, two in ("xy", "yz", "zx"):
        peers += [device(**{one: (place[one] + j) % 4, two: (place[two] + k) % 4})
                  for j in (1, 2, 3) for k in (1, 2, 3)]
    for peer in peers:
        pl.semaphore_signal(barrier, inc=1, device_id=peer, device_id_type=MESH)
    friends = len(peers)
    for dx, dy in SIDES:
        near = halo2.there(dx, dy)
        friends = friends + near.astype(jnp.int32)

        @pl.when(near)
        def _():
            pl.semaphore_signal(barrier, inc=1, device_id={"gx": gx + dx, "gy": gy + dy}, device_id_type=MESH)
    from_z = lax.broadcasted_iota(jnp.int32, sort.shape, 0)
    to_z = lax.broadcasted_iota(jnp.int32, sort.shape, 1)
    sort[...] = jnp.where(from_z == to_z % 128 * 2 + to_z // 128, 1.0, 0.0).astype(BF16)

    def sorted_plane(cells):
        by_row = jnp.swapaxes(cells, 0, 1)
        return nn(by_row.reshape(256, 256), sort[...]).astype(BF16).reshape(by_row.shape)

    loads["g"].wait()
    loads["h_two"].wait()
    for x in range(2):
        masked = jnp.where(h_two_ref[:, x].astype(F32) > 0, g_ref[:, x].astype(F32), 0.0).astype(BF16)
        d2[x + 1, 1:5] = sorted_plane(masked)
        if x == 0:
            pl.semaphore_wait(barrier, friends)
        halo2.start((-1,) if x == 0 else (0, 1))
    for halo in (halo2, halo1, halou, haloc):
        halo.clear()

    loads["c"].wait()
    cb[1, 1:3] = jnp.swapaxes(c_ref[:, 0], 0, 1)
    loads["w2"].wait()
    conv_matrix(w2_ref, rows, a2)
    for name, source, taps, places in (("h", h_ref, h3, (0, 64, 128, 192)), ("up", up_ref, up3, (0, 64, 192, 128))):
        loads[name].wait()
        for x in range(2):
            plane = sorted_plane(source[:, x])
            for y in range(4):
                cells = plane[y]
                wide = cells.astype(F32)
                taps[x, y, places[0] : places[0] + 64] = before(wide).astype(BF16)
                taps[x, y, places[1] : places[1] + 64] = cells
                taps[x, y, places[2] : places[2] + 64] = after(wide).astype(BF16)
                taps[x, y, places[3] : places[3] + 64] = jnp.zeros_like(cells)

    halo2.wait_send()
    haloc.start()

    for x in range(2):
        halo2.wait_recv((0, 1) if x == 0 else (-1,))
        for y in range(4):
            grad = input_rows(a2[...], d2, x, y)
            d1[x + 1, y + 1] = jnp.where(h3[x, y, 64:128].astype(F32) > 0, grad, 0.0).astype(BF16)
        halo1.start((-1,) if x == 0 else (0, 1))

    loads["w1"].wait()
    conv_matrix(w1_ref, rows, a1)
    total2[...] = filter_grad(d2, h3)
    away[0] = total2[rows_at((1 - core) * MIXED_ROWS, MIXED_ROWS)].astype(BF16)
    swaps = [remote(away.at[0], got0.at[0], core_send.at[0], core_recv.at[0], sibling)]
    swaps[0].start()
    haloc.wait_recv()
    swaps.append(remote(cb, cs, core_send.at[1], core_recv.at[1], sibling))
    swaps[1].start()

    def shift_coarse(cells_ref, to_ref):
        for nx, x in enumerate((1, 2 * core)):
            for y in range(4):
                cells = cells_ref[x, y]
                wide = cells.astype(F32)
                to_ref[0, nx, y] = moved(wide, -1).astype(BF16)
                to_ref[1, nx, y] = cells
                to_ref[2, nx, y] = moved(wide, 1).astype(BF16)

    shift_coarse(cb, c3)
    swaps[1].wait_recv()
    shift_coarse(cs, c3s)

    halo1.wait_recv()
    for x in (1 - core, core):
        for y in range(4):
            ub[x + 1, y + 1] = input_rows(a1[...], d1, x, y).astype(BF16)
        if len(swaps) == 2:
            swaps.append(remote(ub.at[x + 1, pl.ds(1, 4)], us, core_send.at[2], core_recv.at[2], sibling))
            swaps[2].start()
    total1[...] = filter_grad(d1, up3)
    away[1] = total1[rows_at((1 - core) * MIXED_ROWS, MIXED_ROWS)].astype(BF16)
    swaps.append(remote(away.at[1], got0.at[1], core_send.at[3], core_recv.at[3], sibling))
    swaps[3].start()

    def ring_start(part):
        axis = ORDERS[part][0]
        copies = []
        for chunk in range(CHUNKS):
            for j in RING:
                to = (place[axis] + j) % 4
                copies.append(remote(
                    held.at[rows_at(part * PART + to * QUARTER + chunk * CHUNK, CHUNK)],
                    got1.at[part, j - 1, pl.ds(chunk * CHUNK, CHUNK)],
                    ring_send.at[0, part, j - 1, chunk], ring_recv.at[0, part, j - 1, chunk], device(**{axis: to})))
                copies[-1].start()
        return copies

    swaps[2].wait_recv()
    fine = (lambda row: ub[1 + core, 1 + row], lambda row: us[row])
    rings = []
    for nx in range(2):
        for py in range(2):
            for pz in range(2):
                result = class_grad(fine, (c3, c3s), nx, py, pz).astype(BF16)
                n = 0
                for ky, _ in tap_choices(py):
                    for kz, _ in tap_choices(pz):
                        to = nx * PART + (4 * ky + kz) * 64
                        held[to : to + 64] = result[:, n * 128 : n * 128 + 128]
                        n += 1
        rings.append(ring_start(nx))
    swaps[0].wait_recv()
    swaps[3].wait_recv()
    mine = rows_at(core * MIXED_ROWS, MIXED_ROWS)
    sum2 = total2[mine] + got0[0].astype(F32)
    sum1 = total1[mine] + got0[1].astype(F32)
    for at, rows_of in enumerate((sum2[:, :128], sum1[:, :128], sum2[:, 128:] + sum1[:, 128:])):
        to = 2 * PART + at * MIXED_ROWS
        held[to : to + MIXED_ROWS] = rows_of.astype(BF16)
    held[2 * PART + 3 * MIXED_ROWS :] = jnp.zeros((PART - 3 * MIXED_ROWS, 128), BF16)
    rings.append(ring_start(2))

    home = [place[ORDERS[part][0]] for part in range(3)]
    seat = [place[ORDERS[part][1]] * 4 + place[ORDERS[part][2]] for part in range(3)]
    start = [core * HALF + part * PART + home[part] * QUARTER for part in range(3)]
    planes = [None] * 3
    for part in (0, 1, 2):
        for copy in rings[part]:
            copy.wait_recv()
        total = held[rows_at(part * PART + home[part] * QUARTER, QUARTER)].astype(F32)
        for j in range(3):
            total = total + got1[part, j].astype(F32)
        own1[part] = total.astype(BF16)
        planes[part] = []
        for j, step in enumerate(PLANE):
            there = plane_place(part, step)
            planes[part].append(remote(own1.at[part, rows_at((there[0] * 4 + there[1]) * PIECE, PIECE)],
                                       got2.at[part, j], plane_send.at[0, part, j], plane_recv.at[0, part, j],
                                       plane_peer(part, step)))
            planes[part][-1].start()
    halou.start()
    sent = rings[0] + rings[1] + rings[2] + planes[0] + planes[1] + planes[2] + swaps

    spread = [None] * 3
    for part in (0, 1, 2):
        for copy in planes[part]:
            copy.wait_recv()
        total = own1[part, rows_at(seat[part] * PIECE, PIECE)].astype(F32)
        for j in range(15):
            total = total + got2[part, j].astype(F32)
        block = out_ref.at[rows_at(start[part] + seat[part] * PIECE, PIECE)]
        out_ref[rows_at(start[part] + seat[part] * PIECE, PIECE)] = total.astype(BF16)
        spread[part] = []
        for j, step in enumerate(PLANE):
            spread[part].append(remote(block, block, plane_send.at[1, part, j], plane_recv.at[1, part, j],
                                       plane_peer(part, step)))
            spread[part][-1].start()
    halou.wait_recv()
    input_grad(ub, wt_ref, loads["wt"], ig_ref)
    shares, writes = [], []

    def write(from_row):
        block = rows_at(from_row, QUARTER)
        writes.append(pltpu.make_async_copy(out_ref.at[block], out_any.at[block], written.at[len(writes)]))
        writes[-1].start()

    def share(from_row):
        block = out_ref.at[rows_at(from_row, QUARTER)]
        at = 4 + len(shares)
        shares.append(remote(block, block, core_send.at[at], core_recv.at[at], sibling))
        shares[-1].start()
        write(from_row)

    back = [None] * 3
    for part in range(3):
        axis = ORDERS[part][0]
        for copy in spread[part]:
            copy.wait_recv()
        back[part] = {j: [] for j in RING}
        for chunk in range(CHUNKS):
            block = out_ref.at[rows_at(start[part] + chunk * CHUNK, CHUNK)]
            for j in RING:
                copy = remote(block, block, ring_send.at[1, part, j - 1, chunk], ring_recv.at[1, part, j - 1, chunk],
                              device(**{axis: (place[axis] + j) % 4}))
                copy.start()
                back[part][j].append(copy)
                sent.append(copy)
        share(start[part])
    for j in (1, 3, 2):
        for part in range(3):
            for copy in back[part][j]:
                copy.wait_recv()
            share(core * HALF + part * PART + (home[part] + 4 - j) % 4 * QUARTER)
    away_rows = (1 - core) * HALF
    order = [(0, part) for part in range(3)] + [(j, part) for j in (1, 3, 2) for part in range(3)]
    for copy, (j, part) in zip(shares, order):
        copy.wait_recv()
        write(away_rows + part * PART + (home[part] + 4 - j) % 4 * QUARTER)
    sent += spread[0] + spread[1] + spread[2] + shares
    for copy in sent:
        copy.wait_send()
    for halo in (halo1, halou, haloc):
        halo.wait_send()
    for copy in writes:
        copy.wait()


def input_grad(ub, wt_ref, load, ig_ref):
    load.wait()
    sums = []
    for half in range(2):
        around = jnp.concatenate(
            [ub[:, 2 * row : 2 * row + 4, :, half * 128 : half * 128 + 128].reshape(1024, 128) for row in range(2)],
            axis=1)
        filters = jnp.concatenate(
            [jnp.concatenate([wt_ref[4 * at + kz] for at in range(16)], axis=0) for kz in (1 - half, 3 - half)], axis=1)
        sums.append(lax.dot_general(filters, around, (((0,), (0,)), ((), ())), preferred_element_type=F32))
    even, odd = sums
    for row in range(2):
        lanes = slice(row * 128, row * 128 + 128)
        ig_ref[row] = (even[:128, lanes] + moved(even[128:, lanes], 1)
                       + odd[128:, lanes] + moved(odd[:128, lanes], -1)).astype(BF16)


def widen(scale, rows_any, ig_rows_any, ig_any, tconv_any, one_any, two_any,
          rows_ref, ig_rows_ref, ig_ref, tconv_ref, one_ref, two_ref, load, done):
    spans = [half * HALF + part * PART for part in range(3) for half in range(2)]
    reads = [pltpu.make_async_copy(rows_any.at[pl.ds(start, PART)], rows_ref.at[pl.ds(start, PART)], load.at[at])
             for at, start in enumerate(spans)]
    reads.append(pltpu.make_async_copy(ig_rows_any, ig_rows_ref, load.at[len(spans)]))
    for copy in reads:
        copy.start()
    writes = []

    def write(source, to):
        writes.append(pltpu.make_async_copy(source, to, done.at[len(writes)]))
        writes[-1].start()

    for at, kx in enumerate((1, 2, 3, 0)):
        reads[at].wait()
        cells = rows_ref[spans[at] : spans[at] + PART].astype(F32) * scale
        tconv_ref[16 * kx : 16 * kx + 16] = cells.reshape(16, 64, 128)
        write(tconv_ref.at[pl.ds(16 * kx, 16)], tconv_any.at[pl.ds(16 * kx, 16)])
    for copy in reads[4:]:
        copy.wait()

    def piece(kind, start, size):
        half, inside = start // MIXED_ROWS, start % MIXED_ROWS
        at = half * HALF + 2 * PART + kind * MIXED_ROWS + inside
        many = min(size, MIXED_ROWS - inside)
        found = rows_ref[at : at + many].astype(F32) * scale
        return found if many == size else jnp.concatenate([found, piece(kind, start + many, size - many)], axis=0)

    for a in range(3):
        for b in range(3):
            low2, low1, high = (piece(kind, ((2 - a) * 3 + 2 - b) * 64, 64) for kind in range(3))
            tap = 9 * a + 3 * b
            two_ref[tap] = low2[:, :64]
            two_ref[tap + 1] = low2[:, 64:]
            two_ref[tap + 2] = high[:, :64]
            one_ref[tap] = low1[:, :64]
            one_ref[tap + 1] = low1[:, 64:]
            one_ref[tap + 2] = high[:, 64:]
    write(two_ref, two_any)
    write(one_ref, one_any)
    ig_ref[:, 0] = jnp.swapaxes(ig_rows_ref[...], 0, 1)
    write(ig_ref, ig_any)
    for copy in writes:
        copy.wait()


def shards(counts, coarse_input, upsampled, hidden_one, hidden_two, cotangent,
           tconv_weight, conv_one_weight, conv_two_weight):
    channels, planes, across, length = cotangent.shape
    scale = 1.0 / math.sqrt(planes * counts[0] * across * counts[1] * length)
    vmem, anywhere = pl.BlockSpec(memory_space=pltpu.VMEM), pl.BlockSpec(memory_space=pl.ANY)
    args = (coarse_input, upsampled, hidden_one, hidden_two, cotangent, tconv_weight, conv_one_weight, conv_two_weight)
    haloed = pltpu.VMEM((4, 6, channels, length), BF16)
    shifted = pltpu.VMEM((2, 4, 256, length), BF16)
    dma = pltpu.SemaphoreType.DMA
    input_rows, total = pl.pallas_call(
        functools.partial(section, counts),
        out_shape=(jax.ShapeDtypeStruct((2, 128, 128), BF16), jax.ShapeDtypeStruct((ROWS, 128), BF16)),
        in_specs=[pl.BlockSpec(memory_space=pltpu.HBM)] * 8,
        out_specs=(vmem, anywhere),
        scratch_shapes=[pltpu.VMEM(arg.shape, arg.dtype) for arg in args] + [
            haloed, haloed, haloed, pltpu.VMEM((3, 4, 128, 128), BF16),
            pltpu.VMEM((4, channels, length), BF16), pltpu.VMEM((3, 4, 128, 128), BF16),
            shifted, shifted, pltpu.VMEM((3, 2, 4, 128, 128), BF16), pltpu.VMEM((3, 2, 4, 128, 128), BF16),
            pltpu.VMEM((CONV_ROWS, 256), BF16), pltpu.VMEM((192, CONV_ROWS), BF16), pltpu.VMEM((192, CONV_ROWS), BF16),
            pltpu.VMEM((length, length), BF16), pltpu.VMEM((CONV_ROWS, 256), F32), pltpu.VMEM((CONV_ROWS, 256), F32),
            pltpu.VMEM((2, MIXED_ROWS, 256), BF16), pltpu.VMEM((2, MIXED_ROWS, 256), BF16),
            pltpu.VMEM((HALF, 128), BF16),
            pltpu.VMEM((3, 3, QUARTER, 128), BF16),
            pltpu.VMEM((3, 15, PIECE, 128), BF16),
            pltpu.VMEM((3, QUARTER, 128), BF16),
            pltpu.VMEM((ROWS, 128), BF16),
            dma((8,)), dma((4, 8)), dma((4, 8)), dma((16,)), dma((16,)),
            dma((2, 3, 3, CHUNKS)), dma((2, 3, 3, CHUNKS)), dma((2, 3, 15)), dma((2, 3, 15)), dma((24,)),
        ],
        compiler_params=pltpu.CompilerParams(collective_id=0, has_side_effects=True, vmem_limit_bytes=VMEM_BYTES),
    )(*args)

    shapes = (((128, 1, 2, 128), BF16), ((64, 64, 128), F32), ((27, 64, 64), F32), ((27, 64, 64), F32))
    return pl.pallas_call(
        functools.partial(widen, scale),
        out_shape=tuple(jax.ShapeDtypeStruct(*shape) for shape in shapes),
        in_specs=[anywhere, anywhere],
        out_specs=(anywhere,) * 4,
        scratch_shapes=[pltpu.VMEM((ROWS, 128), BF16), pltpu.VMEM((2, 128, 128), BF16)]
        + [pltpu.VMEM(*shape) for shape in shapes] + [dma((7,)), dma((7,))],
        compiler_params=pltpu.CompilerParams(vmem_limit_bytes=VMEM_BYTES),
    )(total, input_rows)


def solution(mesh):
    cells = P(None, "gx", "gy", None)
    return jax.shard_map(
        functools.partial(shards, (mesh.shape["gx"], mesh.shape["gy"])),
        mesh=mesh,
        in_specs=(cells,) * 5 + (P(),) * 3,
        out_specs=(cells, P(), P(), P()),
        check_vma=False,
    )
```

```python
import functools
import math

import jax
import jax.numpy as jnp
from jax import lax
from jax.experimental import pallas as pl
from jax.experimental.pallas import tpu as pltpu
from jax.sharding import PartitionSpec as P

BF16 = jnp.bfloat16
F32 = jnp.float32
MESH = pl.DeviceIdType.MESH
SIDES = [(-1, 0), (1, 0), (-1, -1), (1, 1), (-1, 1), (1, -1), (0, -1), (0, 1)]
VMEM_BYTES = 56 * 1024 * 1024

CONV_ROWS = 576
MIXED_ROWS = CONV_ROWS // 2
PART = 1024
HALF = 3 * PART
ROWS = 2 * HALF
QUARTER = PART // 4
PIECE = QUARTER // 16
CHUNKS = 1
CHUNK = QUARTER // CHUNKS
ORDERS = ("xyz", "yzx", "zxy")
RING = (2, 1, 3)
PLANE = sorted(((b, c) for b in range(4) for c in range(4) if b or c), key=lambda s: -min(s[0], 4 - s[0]) - min(s[1], 4 - s[1]))


def nn(a, b):
    return lax.dot_general(a, b, (((1,), (0,)), ((), ())), preferred_element_type=F32)


def nt(a, b):
    return lax.dot_general(a, b, (((1,), (1,)), ((), ())), preferred_element_type=F32)


def moved(cells, by):
    length = cells.shape[-1]
    lane = lax.broadcasted_iota(jnp.int32, cells.shape, cells.ndim - 1)
    rolled = pltpu.roll(cells, (-by) % length, cells.ndim - 1)
    return jnp.where(lane == (0 if by < 0 else length - 1), 0.0, rolled)


def exists(gx, gy, dx, dy, count_x, count_y):
    found = []
    if dx < 0:
        found.append(gx > 0)
    if dx > 0:
        found.append(gx < count_x - 1)
    if dy < 0:
        found.append(gy > 0)
    if dy > 0:
        found.append(gy < count_y - 1)
    return functools.reduce(jnp.logical_and, found)


class Halo:
    def __init__(self, buf, send, recv, counts):
        self.buf, self.send, self.recv, self.counts = buf, send, recv, counts
        self.planes, self.rows = buf.shape[0] - 2, buf.shape[1] - 2
        self.gx, self.gy = lax.axis_index("gx"), lax.axis_index("gy")

    def clear(self):
        ends = ((self.gx == 0, 0, None), (self.gx == self.counts[0] - 1, self.planes + 1, None),
                (self.gy == 0, None, 0), (self.gy == self.counts[1] - 1, None, self.rows + 1))
        for at_end, plane, row in ends:
            @pl.when(at_end)
            def _():
                if plane is not None:
                    self.buf[plane] = jnp.zeros(self.buf.shape[1:], BF16)
                else:
                    self.buf[:, row] = jnp.zeros(self.buf.shape[:1] + self.buf.shape[2:], BF16)

    def copy(self, k):
        dx, dy = SIDES[k]

        def cut(step, size):
            if step == 0:
                return (1, 1, size)
            return (1, size + 1, 1) if step < 0 else (size, 0, 1)

        from_x, to_x, many_x = cut(dx, self.planes)
        from_y, to_y, many_y = cut(dy, self.rows)
        return pltpu.make_async_remote_copy(
            src_ref=self.buf.at[pl.ds(from_x, many_x), pl.ds(from_y, many_y)],
            dst_ref=self.buf.at[pl.ds(to_x, many_x), pl.ds(to_y, many_y)],
            send_sem=self.send.at[k],
            recv_sem=self.recv.at[k],
            device_id={"gx": self.gx + dx, "gy": self.gy + dy},
            device_id_type=MESH,
        )

    def there(self, dx, dy):
        return exists(self.gx, self.gy, dx, dy, *self.counts)

    def start(self, steps=(-1, 0, 1)):
        for k, (dx, dy) in enumerate(SIDES):
            if dx not in steps:
                continue

            @pl.when(self.there(dx, dy))
            def _():
                self.copy(k).start()

    def wait_recv(self, steps=(-1, 0, 1)):
        for k, (dx, dy) in enumerate(SIDES):
            if dx not in steps:
                continue

            @pl.when(self.there(-dx, -dy))
            def _():
                self.copy(k).wait_recv()

    def wait_send(self):
        for k, (dx, dy) in enumerate(SIDES):
            @pl.when(self.there(dx, dy))
            def _():
                self.copy(k).wait_send()


def before(cells):
    half = cells.shape[-1] // 2
    return jnp.concatenate([moved(cells[..., half:], -1), cells[..., :half]], axis=-1)


def after(cells):
    half = cells.shape[-1] // 2
    return jnp.concatenate([cells[..., half:], moved(cells[..., :half], 1)], axis=-1)


def input_rows(weights, halo_ref, x, y):
    window = halo_ref[pl.ds(x, 3), y : y + 3].reshape(weights.shape[1], halo_ref.shape[3])
    taps = nn(weights, window)
    size = taps.shape[0] // 3
    return after(taps[:size]) + taps[size : 2 * size] + before(taps[2 * size :])


def filter_grad(halo_ref, taps_ref):
    rows = [(x, y) for x in range(2) for y in range(4)]
    windows = [halo_ref[x : x + 3, y : y + 3].reshape(CONV_ROWS, halo_ref.shape[3]) for x, y in rows]
    return nt(jnp.concatenate(windows, axis=1), jnp.concatenate([taps_ref[x, y] for x, y in rows], axis=1))


def conv_matrix(weight_ref, rows_ref, matrix_ref):
    rows_ref[:, 192:] = jnp.zeros((CONV_ROWS, 64), BF16)
    for a in range(3):
        for b in range(3):
            at = ((2 - a) * 3 + 2 - b) * 64
            for c in range(3):
                rows_ref[at : at + 64, c * 64 : c * 64 + 64] = weight_ref[9 * a + 3 * b + c]
    matrix_ref[...] = rows_ref[...].T[:192]


def tap_choices(parity):
    return ((2, 1), (0, 2)) if parity else ((1, 1), (3, 0))


def class_grad(fine, coarse, nx, py, pz):
    own = jnp.concatenate(
        [cells(2 * row + py)[:, pz * 128 : pz * 128 + 128] for cells in fine for row in range(2)], axis=1)
    parts = []
    for _, sy in tap_choices(py):
        for _, sz in tap_choices(pz):
            parts.append(jnp.concatenate([c3[sz, nx, row + sy] for c3 in coarse for row in range(2)], axis=1))
    return nt(own, jnp.concatenate(parts, axis=0))


def section(counts, c_any, up_any, h_any, h_two_any, g_any, wt_any, w1_any, w2_any, ig_ref, out_any,
            c_ref, up_ref, h_ref, h_two_ref, g_ref, wt_ref, w1_ref, w2_ref,
            d2, d1, ub, cb, us, cs, h3, up3, c3, c3s, rows, a2, a1, sort, total2, total1, away, got0,
            held, got1, got2, own1, out_ref,
            load, halo_send, halo_recv, core_send, core_recv, ring_send, ring_recv, plane_send, plane_recv, written):
    loads = {}
    for at, (name, source, to) in enumerate((
            ("g", g_any, g_ref), ("h_two", h_two_any, h_two_ref), ("c", c_any, c_ref), ("w2", w2_any, w2_ref),
            ("h", h_any, h_ref), ("up", up_any, up_ref), ("w1", w1_any, w1_ref), ("wt", wt_any, wt_ref))):
        loads[name] = pltpu.make_async_copy(source, to, load.at[at])
        loads[name].start()

    gx, gy = lax.axis_index("gx"), lax.axis_index("gy")
    place = {"x": gx % 4, "z": gx // 4 % 4, "y": gx // 16 * 2 + gy // 2}
    core = gy % 2

    def device(**moves):
        spot = {**place, **moves}
        return {"gx": spot["y"] // 2 * 16 + spot["z"] * 4 + spot["x"], "gy": spot["y"] % 2 * 2 + core}

    sibling = {"gx": gx, "gy": gy - core + 1 - core}

    def remote(src, dst, send_sem, recv_sem, peer):
        return pltpu.make_async_remote_copy(src_ref=src, dst_ref=dst, send_sem=send_sem, recv_sem=recv_sem,
                                            device_id=peer, device_id_type=MESH)

    def rows_at(start, size):
        return pl.ds(pl.multiple_of(start, 16), size)

    def plane_place(part, step):
        return [(place[axis] + by) % 4 for axis, by in zip(ORDERS[part][1:], step)]

    def plane_peer(part, step):
        return device(**dict(zip(ORDERS[part][1:], plane_place(part, step))))

    halo2, halo1, halou, haloc = (
        Halo(buf, halo_send.at[at], halo_recv.at[at], counts) for at, buf in enumerate((d2, d1, ub, cb)))
    barrier = pltpu.get_barrier_semaphore()
    peers = [sibling] + [device(**{axis: (place[axis] + j) % 4}) for axis in "xyz" for j in (1, 2, 3)]
    for one, two in ("xy", "yz", "zx"):
        peers += [device(**{one: (place[one] + j) % 4, two: (place[two] + k) % 4})
                  for j in (1, 2, 3) for k in (1, 2, 3)]
    for peer in peers:
        pl.semaphore_signal(barrier, inc=1, device_id=peer, device_id_type=MESH)
    friends = len(peers)
    for dx, dy in SIDES:
        near = halo2.there(dx, dy)
        friends = friends + near.astype(jnp.int32)

        @pl.when(near)
        def _():
            pl.semaphore_signal(barrier, inc=1, device_id={"gx": gx + dx, "gy": gy + dy}, device_id_type=MESH)
    from_z = lax.broadcasted_iota(jnp.int32, sort.shape, 0)
    to_z = lax.broadcasted_iota(jnp.int32, sort.shape, 1)
    sort[...] = jnp.where(from_z == to_z % 128 * 2 + to_z // 128, 1.0, 0.0).astype(BF16)

    def sorted_plane(cells):
        by_row = jnp.swapaxes(cells, 0, 1)
        return nn(by_row.reshape(256, 256), sort[...]).astype(BF16).reshape(by_row.shape)

    loads["g"].wait()
    loads["h_two"].wait()
    for x in range(2):
        masked = jnp.where(h_two_ref[:, x].astype(F32) > 0, g_ref[:, x].astype(F32), 0.0).astype(BF16)
        d2[x + 1, 1:5] = sorted_plane(masked)
        if x == 0:
            pl.semaphore_wait(barrier, friends)
        halo2.start((-1,) if x == 0 else (0, 1))
    for halo in (halo2, halo1, halou, haloc):
        halo.clear()

    loads["c"].wait()
    cb[1, 1:3] = jnp.swapaxes(c_ref[:, 0], 0, 1)
    loads["w2"].wait()
    conv_matrix(w2_ref, rows, a2)
    for name, source, taps, places in (("h", h_ref, h3, (0, 64, 128, 192)), ("up", up_ref, up3, (0, 64, 192, 128))):
        loads[name].wait()
        for x in range(2):
            plane = sorted_plane(source[:, x])
            for y in range(4):
                cells = plane[y]
                wide = cells.astype(F32)
                taps[x, y, places[0] : places[0] + 64] = before(wide).astype(BF16)
                taps[x, y, places[1] : places[1] + 64] = cells
                taps[x, y, places[2] : places[2] + 64] = after(wide).astype(BF16)
                taps[x, y, places[3] : places[3] + 64] = jnp.zeros_like(cells)

    halo2.wait_send()
    haloc.start()

    for x in range(2):
        halo2.wait_recv((0, 1) if x == 0 else (-1,))
        for y in range(4):
            grad = input_rows(a2[...], d2, x, y)
            d1[x + 1, y + 1] = jnp.where(h3[x, y, 64:128].astype(F32) > 0, grad, 0.0).astype(BF16)
        halo1.start((-1,) if x == 0 else (0, 1))

    loads["w1"].wait()
    conv_matrix(w1_ref, rows, a1)
    total2[...] = filter_grad(d2, h3)
    away[0] = total2[rows_at((1 - core) * MIXED_ROWS, MIXED_ROWS)].astype(BF16)
    swaps = [remote(away.at[0], got0.at[0], core_send.at[0], core_recv.at[0], sibling)]
    swaps[0].start()
    haloc.wait_recv()
    swaps.append(remote(cb, cs, core_send.at[1], core_recv.at[1], sibling))
    swaps[1].start()

    def shift_coarse(cells_ref, to_ref):
        for nx, x in enumerate((1, 2 * core)):
            for y in range(4):
                cells = cells_ref[x, y]
                wide = cells.astype(F32)
                to_ref[0, nx, y] = moved(wide, -1).astype(BF16)
                to_ref[1, nx, y] = cells
                to_ref[2, nx, y] = moved(wide, 1).astype(BF16)

    shift_coarse(cb, c3)
    swaps[1].wait_recv()
    shift_coarse(cs, c3s)

    halo1.wait_recv()
    for x in (1 - core, core):
        for y in range(4):
            ub[x + 1, y + 1] = input_rows(a1[...], d1, x, y).astype(BF16)
        if len(swaps) == 2:
            swaps.append(remote(ub.at[x + 1, pl.ds(1, 4)], us, core_send.at[2], core_recv.at[2], sibling))
            swaps[2].start()
    total1[...] = filter_grad(d1, up3)
    away[1] = total1[rows_at((1 - core) * MIXED_ROWS, MIXED_ROWS)].astype(BF16)
    swaps.append(remote(away.at[1], got0.at[1], core_send.at[3], core_recv.at[3], sibling))
    swaps[3].start()

    def ring_start(part):
        axis = ORDERS[part][0]
        copies = []
        for chunk in range(CHUNKS):
            for j in RING:
                to = (place[axis] + j) % 4
                copies.append(remote(
                    held.at[rows_at(part * PART + to * QUARTER + chunk * CHUNK, CHUNK)],
                    got1.at[part, j - 1, pl.ds(chunk * CHUNK, CHUNK)],
                    ring_send.at[0, part, j - 1, chunk], ring_recv.at[0, part, j - 1, chunk], device(**{axis: to})))
                copies[-1].start()
        return copies

    swaps[2].wait_recv()
    fine = (lambda row: ub[1 + core, 1 + row], lambda row: us[row])
    rings = []
    for nx in range(2):
        for py in range(2):
            for pz in range(2):
                result = class_grad(fine, (c3, c3s), nx, py, pz).astype(BF16)
                n = 0
                for ky, _ in tap_choices(py):
                    for kz, _ in tap_choices(pz):
                        to = nx * PART + (4 * ky + kz) * 64
                        held[to : to + 64] = result[:, n * 128 : n * 128 + 128]
                        n += 1
        rings.append(ring_start(nx))
    swaps[0].wait_recv()
    swaps[3].wait_recv()
    mine = rows_at(core * MIXED_ROWS, MIXED_ROWS)
    sum2 = total2[mine] + got0[0].astype(F32)
    sum1 = total1[mine] + got0[1].astype(F32)
    for at, rows_of in enumerate((sum2[:, :128], sum1[:, :128], sum2[:, 128:] + sum1[:, 128:])):
        to = 2 * PART + at * MIXED_ROWS
        held[to : to + MIXED_ROWS] = rows_of.astype(BF16)
    held[2 * PART + 3 * MIXED_ROWS :] = jnp.zeros((PART - 3 * MIXED_ROWS, 128), BF16)
    rings.append(ring_start(2))

    home = [place[ORDERS[part][0]] for part in range(3)]
    seat = [place[ORDERS[part][1]] * 4 + place[ORDERS[part][2]] for part in range(3)]
    start = [core * HALF + part * PART + home[part] * QUARTER for part in range(3)]
    planes = [None] * 3
    for part in (0, 1, 2):
        for copy in rings[part]:
            copy.wait_recv()
        total = held[rows_at(part * PART + home[part] * QUARTER, QUARTER)].astype(F32)
        for j in range(3):
            total = total + got1[part, j].astype(F32)
        own1[part] = total.astype(BF16)
        planes[part] = []
        for j, step in enumerate(PLANE):
            there = plane_place(part, step)
            planes[part].append(remote(own1.at[part, rows_at((there[0] * 4 + there[1]) * PIECE, PIECE)],
                                       got2.at[part, j], plane_send.at[0, part, j], plane_recv.at[0, part, j],
                                       plane_peer(part, step)))
            planes[part][-1].start()
    sent = rings[0] + rings[1] + rings[2] + planes[0] + planes[1] + planes[2] + swaps

    spread = [None] * 3
    for part in (0, 1, 2):
        for copy in planes[part]:
            copy.wait_recv()
        total = own1[part, rows_at(seat[part] * PIECE, PIECE)].astype(F32)
        for j in range(15):
            total = total + got2[part, j].astype(F32)
        block = out_ref.at[rows_at(start[part] + seat[part] * PIECE, PIECE)]
        out_ref[rows_at(start[part] + seat[part] * PIECE, PIECE)] = total.astype(BF16)
        spread[part] = []
        for j, step in enumerate(PLANE):
            spread[part].append(remote(block, block, plane_send.at[1, part, j], plane_recv.at[1, part, j],
                                       plane_peer(part, step)))
            spread[part][-1].start()
    halou.start()
    shares, writes = [], []

    def write(from_row):
        block = rows_at(from_row, QUARTER)
        writes.append(pltpu.make_async_copy(out_ref.at[block], out_any.at[block], written.at[len(writes)]))
        writes[-1].start()

    def share(from_row):
        block = out_ref.at[rows_at(from_row, QUARTER)]
        at = 4 + len(shares)
        shares.append(remote(block, block, core_send.at[at], core_recv.at[at], sibling))
        shares[-1].start()
        write(from_row)

    back = [None] * 3
    for part in range(3):
        axis = ORDERS[part][0]
        for copy in spread[part]:
            copy.wait_recv()
        back[part] = {j: [] for j in RING}
        for chunk in range(CHUNKS):
            block = out_ref.at[rows_at(start[part] + chunk * CHUNK, CHUNK)]
            for j in RING:
                copy = remote(block, block, ring_send.at[1, part, j - 1, chunk], ring_recv.at[1, part, j - 1, chunk],
                              device(**{axis: (place[axis] + j) % 4}))
                copy.start()
                back[part][j].append(copy)
                sent.append(copy)
        share(start[part])
    halou.wait_recv()
    input_grad(ub, wt_ref, loads["wt"], ig_ref)
    for j in (1, 3, 2):
        for part in range(3):
            for copy in back[part][j]:
                copy.wait_recv()
            share(core * HALF + part * PART + (home[part] + 4 - j) % 4 * QUARTER)
    away_rows = (1 - core) * HALF
    order = [(0, part) for part in range(3)] + [(j, part) for j in (1, 3, 2) for part in range(3)]
    for copy, (j, part) in zip(shares, order):
        copy.wait_recv()
        write(away_rows + part * PART + (home[part] + 4 - j) % 4 * QUARTER)
    sent += spread[0] + spread[1] + spread[2] + shares
    for copy in sent:
        copy.wait_send()
    for halo in (halo1, halou, haloc):
        halo.wait_send()
    for copy in writes:
        copy.wait()


def input_grad(ub, wt_ref, load, ig_ref):
    load.wait()
    sums = []
    for half in range(2):
        around = jnp.concatenate(
            [ub[:, 2 * row : 2 * row + 4, :, half * 128 : half * 128 + 128].reshape(1024, 128) for row in range(2)],
            axis=1)
        filters = jnp.concatenate(
            [jnp.concatenate([wt_ref[4 * at + kz] for at in range(16)], axis=0) for kz in (1 - half, 3 - half)], axis=1)
        sums.append(lax.dot_general(filters, around, (((0,), (0,)), ((), ())), preferred_element_type=F32))
    even, odd = sums
    for row in range(2):
        lanes = slice(row * 128, row * 128 + 128)
        ig_ref[row] = (even[:128, lanes] + moved(even[128:, lanes], 1)
                       + odd[128:, lanes] + moved(odd[:128, lanes], -1)).astype(BF16)


def widen(scale, rows_any, ig_rows_any, ig_any, tconv_any, one_any, two_any,
          rows_ref, ig_rows_ref, ig_ref, tconv_ref, one_ref, two_ref, load, done):
    spans = [half * HALF + part * PART for part in (2, 0, 1) for half in range(2)]
    reads = [pltpu.make_async_copy(rows_any.at[pl.ds(start, PART)], rows_ref.at[pl.ds(start, PART)], load.at[at])
             for at, start in enumerate(spans)]
    reads.append(pltpu.make_async_copy(ig_rows_any, ig_rows_ref, load.at[len(spans)]))
    for copy in reads:
        copy.start()
    writes = []

    def write(source, to):
        writes.append(pltpu.make_async_copy(source, to, done.at[len(writes)]))
        writes[-1].start()

    for copy in reads[:2]:
        copy.wait()

    def piece(kind, start, size):
        half, inside = start // MIXED_ROWS, start % MIXED_ROWS
        at = half * HALF + 2 * PART + kind * MIXED_ROWS + inside
        many = min(size, MIXED_ROWS - inside)
        found = rows_ref[at : at + many].astype(F32) * scale
        return found if many == size else jnp.concatenate([found, piece(kind, start + many, size - many)], axis=0)

    for a in range(3):
        for b in range(3):
            low2, low1, high = (piece(kind, ((2 - a) * 3 + 2 - b) * 64, 64) for kind in range(3))
            tap = 9 * a + 3 * b
            two_ref[tap] = low2[:, :64]
            two_ref[tap + 1] = low2[:, 64:]
            two_ref[tap + 2] = high[:, :64]
            one_ref[tap] = low1[:, :64]
            one_ref[tap + 1] = low1[:, 64:]
            one_ref[tap + 2] = high[:, 64:]
    write(two_ref, two_any)
    write(one_ref, one_any)
    for at, kx in enumerate((1, 2, 3, 0), 2):
        reads[at].wait()
        cells = rows_ref[spans[at] : spans[at] + PART].astype(F32) * scale
        tconv_ref[16 * kx : 16 * kx + 16] = cells.reshape(16, 64, 128)
        write(tconv_ref.at[pl.ds(16 * kx, 16)], tconv_any.at[pl.ds(16 * kx, 16)])
    reads[6].wait()
    ig_ref[:, 0] = jnp.swapaxes(ig_rows_ref[...], 0, 1)
    write(ig_ref, ig_any)
    for copy in writes:
        copy.wait()


def shards(counts, coarse_input, upsampled, hidden_one, hidden_two, cotangent,
           tconv_weight, conv_one_weight, conv_two_weight):
    channels, planes, across, length = cotangent.shape
    scale = 1.0 / math.sqrt(planes * counts[0] * across * counts[1] * length)
    vmem, anywhere = pl.BlockSpec(memory_space=pltpu.VMEM), pl.BlockSpec(memory_space=pl.ANY)
    args = (coarse_input, upsampled, hidden_one, hidden_two, cotangent, tconv_weight, conv_one_weight, conv_two_weight)
    haloed = pltpu.VMEM((4, 6, channels, length), BF16)
    shifted = pltpu.VMEM((2, 4, 256, length), BF16)
    dma = pltpu.SemaphoreType.DMA
    input_rows, total = pl.pallas_call(
        functools.partial(section, counts),
        out_shape=(jax.ShapeDtypeStruct((2, 128, 128), BF16), jax.ShapeDtypeStruct((ROWS, 128), BF16)),
        in_specs=[pl.BlockSpec(memory_space=pltpu.HBM)] * 8,
        out_specs=(vmem, anywhere),
        scratch_shapes=[pltpu.VMEM(arg.shape, arg.dtype) for arg in args] + [
            haloed, haloed, haloed, pltpu.VMEM((3, 4, 128, 128), BF16),
            pltpu.VMEM((4, channels, length), BF16), pltpu.VMEM((3, 4, 128, 128), BF16),
            shifted, shifted, pltpu.VMEM((3, 2, 4, 128, 128), BF16), pltpu.VMEM((3, 2, 4, 128, 128), BF16),
            pltpu.VMEM((CONV_ROWS, 256), BF16), pltpu.VMEM((192, CONV_ROWS), BF16), pltpu.VMEM((192, CONV_ROWS), BF16),
            pltpu.VMEM((length, length), BF16), pltpu.VMEM((CONV_ROWS, 256), F32), pltpu.VMEM((CONV_ROWS, 256), F32),
            pltpu.VMEM((2, MIXED_ROWS, 256), BF16), pltpu.VMEM((2, MIXED_ROWS, 256), BF16),
            pltpu.VMEM((HALF, 128), BF16),
            pltpu.VMEM((3, 3, QUARTER, 128), BF16),
            pltpu.VMEM((3, 15, PIECE, 128), BF16),
            pltpu.VMEM((3, QUARTER, 128), BF16),
            pltpu.VMEM((ROWS, 128), BF16),
            dma((8,)), dma((4, 8)), dma((4, 8)), dma((16,)), dma((16,)),
            dma((2, 3, 3, CHUNKS)), dma((2, 3, 3, CHUNKS)), dma((2, 3, 15)), dma((2, 3, 15)), dma((24,)),
        ],
        compiler_params=pltpu.CompilerParams(collective_id=0, has_side_effects=True, vmem_limit_bytes=VMEM_BYTES),
    )(*args)

    shapes = (((128, 1, 2, 128), BF16), ((64, 64, 128), F32), ((27, 64, 64), F32), ((27, 64, 64), F32))
    return pl.pallas_call(
        functools.partial(widen, scale),
        out_shape=tuple(jax.ShapeDtypeStruct(*shape) for shape in shapes),
        in_specs=[anywhere, anywhere],
        out_specs=(anywhere,) * 4,
        scratch_shapes=[pltpu.VMEM((ROWS, 128), BF16), pltpu.VMEM((2, 128, 128), BF16)]
        + [pltpu.VMEM(*shape) for shape in shapes] + [dma((7,)), dma((7,))],
        compiler_params=pltpu.CompilerParams(vmem_limit_bytes=VMEM_BYTES),
    )(total, input_rows)


def solution(mesh):
    cells = P(None, "gx", "gy", None)
    return jax.shard_map(
        functools.partial(shards, (mesh.shape["gx"], mesh.shape["gy"])),
        mesh=mesh,
        in_specs=(cells,) * 5 + (P(),) * 3,
        out_specs=(cells, P(), P(), P()),
        check_vma=False,
    )
```

```python
import functools
import math

import jax
import jax.numpy as jnp
from jax import lax
from jax.experimental import pallas as pl
from jax.experimental.pallas import tpu as pltpu
from jax.sharding import PartitionSpec as P

BF16 = jnp.bfloat16
F32 = jnp.float32
MESH = pl.DeviceIdType.MESH
SIDES = [(-1, 0), (1, 0), (-1, -1), (1, 1), (-1, 1), (1, -1), (0, -1), (0, 1)]
VMEM_BYTES = 56 * 1024 * 1024

CONV_ROWS = 576
MIXED_ROWS = CONV_ROWS // 2
PART = 1024
HALF = 3 * PART
ROWS = 2 * HALF
QUARTER = PART // 4
PIECE = QUARTER // 16
CHUNKS = 1
CHUNK = QUARTER // CHUNKS
ORDERS = ("xyz", "yzx", "zxy")
RING = (2, 1, 3)
PLANE = sorted(((b, c) for b in range(4) for c in range(4) if b or c), key=lambda s: -min(s[0], 4 - s[0]) - min(s[1], 4 - s[1]))


def nn(a, b):
    return lax.dot_general(a, b, (((1,), (0,)), ((), ())), preferred_element_type=F32)


def nt(a, b):
    return lax.dot_general(a, b, (((1,), (1,)), ((), ())), preferred_element_type=F32)


def moved(cells, by):
    length = cells.shape[-1]
    lane = lax.broadcasted_iota(jnp.int32, cells.shape, cells.ndim - 1)
    rolled = pltpu.roll(cells, (-by) % length, cells.ndim - 1)
    return jnp.where(lane == (0 if by < 0 else length - 1), 0.0, rolled)


def exists(gx, gy, dx, dy, count_x, count_y):
    found = []
    if dx < 0:
        found.append(gx > 0)
    if dx > 0:
        found.append(gx < count_x - 1)
    if dy < 0:
        found.append(gy > 0)
    if dy > 0:
        found.append(gy < count_y - 1)
    return functools.reduce(jnp.logical_and, found)


class Halo:
    def __init__(self, buf, send, recv, counts):
        self.buf, self.send, self.recv, self.counts = buf, send, recv, counts
        self.planes, self.rows = buf.shape[0] - 2, buf.shape[1] - 2
        self.gx, self.gy = lax.axis_index("gx"), lax.axis_index("gy")

    def clear(self):
        ends = ((self.gx == 0, 0, None), (self.gx == self.counts[0] - 1, self.planes + 1, None),
                (self.gy == 0, None, 0), (self.gy == self.counts[1] - 1, None, self.rows + 1))
        for at_end, plane, row in ends:
            @pl.when(at_end)
            def _():
                if plane is not None:
                    self.buf[plane] = jnp.zeros(self.buf.shape[1:], BF16)
                else:
                    self.buf[:, row] = jnp.zeros(self.buf.shape[:1] + self.buf.shape[2:], BF16)

    def copy(self, k):
        dx, dy = SIDES[k]

        def cut(step, size):
            if step == 0:
                return (1, 1, size)
            return (1, size + 1, 1) if step < 0 else (size, 0, 1)

        from_x, to_x, many_x = cut(dx, self.planes)
        from_y, to_y, many_y = cut(dy, self.rows)
        return pltpu.make_async_remote_copy(
            src_ref=self.buf.at[pl.ds(from_x, many_x), pl.ds(from_y, many_y)],
            dst_ref=self.buf.at[pl.ds(to_x, many_x), pl.ds(to_y, many_y)],
            send_sem=self.send.at[k],
            recv_sem=self.recv.at[k],
            device_id={"gx": self.gx + dx, "gy": self.gy + dy},
            device_id_type=MESH,
        )

    def there(self, dx, dy):
        return exists(self.gx, self.gy, dx, dy, *self.counts)

    def start(self, steps=(-1, 0, 1)):
        for k, (dx, dy) in enumerate(SIDES):
            if dx not in steps:
                continue

            @pl.when(self.there(dx, dy))
            def _():
                self.copy(k).start()

    def wait_recv(self, steps=(-1, 0, 1)):
        for k, (dx, dy) in enumerate(SIDES):
            if dx not in steps:
                continue

            @pl.when(self.there(-dx, -dy))
            def _():
                self.copy(k).wait_recv()

    def wait_send(self):
        for k, (dx, dy) in enumerate(SIDES):
            @pl.when(self.there(dx, dy))
            def _():
                self.copy(k).wait_send()


def before(cells):
    half = cells.shape[-1] // 2
    return jnp.concatenate([moved(cells[..., half:], -1), cells[..., :half]], axis=-1)


def after(cells):
    half = cells.shape[-1] // 2
    return jnp.concatenate([cells[..., half:], moved(cells[..., :half], 1)], axis=-1)


def input_rows(weights, halo_ref, x, y):
    window = halo_ref[pl.ds(x, 3), y : y + 3].reshape(weights.shape[1], halo_ref.shape[3])
    taps = nn(weights, window)
    size = taps.shape[0] // 3
    return after(taps[:size]) + taps[size : 2 * size] + before(taps[2 * size :])


def filter_grad(halo_ref, taps_ref):
    rows = [(x, y) for x in range(2) for y in range(4)]
    windows = [halo_ref[x : x + 3, y : y + 3].reshape(CONV_ROWS, halo_ref.shape[3]) for x, y in rows]
    return nt(jnp.concatenate(windows, axis=1), jnp.concatenate([taps_ref[x, y] for x, y in rows], axis=1))


def conv_matrix(weight_ref, rows_ref, matrix_ref):
    rows_ref[:, 192:] = jnp.zeros((CONV_ROWS, 64), BF16)
    for a in range(3):
        for b in range(3):
            at = ((2 - a) * 3 + 2 - b) * 64
            for c in range(3):
                rows_ref[at : at + 64, c * 64 : c * 64 + 64] = weight_ref[9 * a + 3 * b + c]
    matrix_ref[...] = rows_ref[...].T[:192]


def tap_choices(parity):
    return ((2, 1), (0, 2)) if parity else ((1, 1), (3, 0))


def class_grad(fine, coarse, nx, py, pz):
    own = jnp.concatenate(
        [cells(2 * row + py)[:, pz * 128 : pz * 128 + 128] for cells in fine for row in range(2)], axis=1)
    parts = []
    for _, sy in tap_choices(py):
        for _, sz in tap_choices(pz):
            parts.append(jnp.concatenate([c3[sz, nx, row + sy] for c3 in coarse for row in range(2)], axis=1))
    return nt(own, jnp.concatenate(parts, axis=0))


def section(counts, c_any, up_any, h_any, h_two_any, g_any, wt_any, w1_any, w2_any, ig_ref, out_any,
            c_ref, up_ref, h_ref, h_two_ref, g_ref, wt_ref, w1_ref, w2_ref,
            d2, d1, ub, cb, us, cs, h3, up3, c3, c3s, rows, a2, a1, sort, total2, total1, away, got0,
            held, got1, got2, own1, out_ref,
            load, halo_send, halo_recv, core_send, core_recv, ring_send, ring_recv, plane_send, plane_recv, written):
    loads = {}
    for at, (name, source, to) in enumerate((
            ("g", g_any, g_ref), ("h_two", h_two_any, h_two_ref), ("c", c_any, c_ref), ("w2", w2_any, w2_ref),
            ("h", h_any, h_ref), ("up", up_any, up_ref), ("w1", w1_any, w1_ref), ("wt", wt_any, wt_ref))):
        loads[name] = pltpu.make_async_copy(source, to, load.at[at])
        loads[name].start()

    gx, gy = lax.axis_index("gx"), lax.axis_index("gy")
    place = {"x": gx % 4, "z": gx // 4 % 4, "y": gx // 16 * 2 + gy // 2}
    core = gy % 2

    def device(**moves):
        spot = {**place, **moves}
        return {"gx": spot["y"] // 2 * 16 + spot["z"] * 4 + spot["x"], "gy": spot["y"] % 2 * 2 + core}

    sibling = {"gx": gx, "gy": gy - core + 1 - core}

    def remote(src, dst, send_sem, recv_sem, peer):
        return pltpu.make_async_remote_copy(src_ref=src, dst_ref=dst, send_sem=send_sem, recv_sem=recv_sem,
                                            device_id=peer, device_id_type=MESH)

    def rows_at(start, size):
        return pl.ds(pl.multiple_of(start, 16), size)

    def plane_place(part, step):
        return [(place[axis] + by) % 4 for axis, by in zip(ORDERS[part][1:], step)]

    def plane_peer(part, step):
        return device(**dict(zip(ORDERS[part][1:], plane_place(part, step))))

    halo2, halo1, halou, haloc = (
        Halo(buf, halo_send.at[at], halo_recv.at[at], counts) for at, buf in enumerate((d2, d1, ub, cb)))
    barrier = pltpu.get_barrier_semaphore()
    peers = [sibling] + [device(**{axis: (place[axis] + j) % 4}) for axis in "xyz" for j in (1, 2, 3)]
    for one, two in ("xy", "yz", "zx"):
        peers += [device(**{one: (place[one] + j) % 4, two: (place[two] + k) % 4})
                  for j in (1, 2, 3) for k in (1, 2, 3)]
    for peer in peers:
        pl.semaphore_signal(barrier, inc=1, device_id=peer, device_id_type=MESH)
    friends = len(peers)
    for dx, dy in SIDES:
        near = halo2.there(dx, dy)
        friends = friends + near.astype(jnp.int32)

        @pl.when(near)
        def _():
            pl.semaphore_signal(barrier, inc=1, device_id={"gx": gx + dx, "gy": gy + dy}, device_id_type=MESH)
    from_z = lax.broadcasted_iota(jnp.int32, sort.shape, 0)
    to_z = lax.broadcasted_iota(jnp.int32, sort.shape, 1)
    sort[...] = jnp.where(from_z == to_z % 128 * 2 + to_z // 128, 1.0, 0.0).astype(BF16)

    def sorted_plane(cells):
        by_row = jnp.swapaxes(cells, 0, 1)
        return nn(by_row.reshape(256, 256), sort[...]).astype(BF16).reshape(by_row.shape)

    loads["g"].wait()
    loads["h_two"].wait()
    for x in range(2):
        masked = jnp.where(h_two_ref[:, x].astype(F32) > 0, g_ref[:, x].astype(F32), 0.0).astype(BF16)
        d2[x + 1, 1:5] = sorted_plane(masked)
        if x == 0:
            pl.semaphore_wait(barrier, friends)
        halo2.start((-1,) if x == 0 else (0, 1))
    for halo in (halo2, halo1, halou, haloc):
        halo.clear()

    loads["c"].wait()
    cb[1, 1:3] = jnp.swapaxes(c_ref[:, 0], 0, 1)
    loads["w2"].wait()
    conv_matrix(w2_ref, rows, a2)
    for name, source, taps, places in (("h", h_ref, h3, (0, 64, 128, 192)), ("up", up_ref, up3, (0, 64, 192, 128))):
        loads[name].wait()
        for x in range(2):
            plane = sorted_plane(source[:, x])
            for y in range(4):
                cells = plane[y]
                wide = cells.astype(F32)
                taps[x, y, places[0] : places[0] + 64] = before(wide).astype(BF16)
                taps[x, y, places[1] : places[1] + 64] = cells
                taps[x, y, places[2] : places[2] + 64] = after(wide).astype(BF16)
                taps[x, y, places[3] : places[3] + 64] = jnp.zeros_like(cells)

    halo2.wait_send()
    haloc.start()

    for x in range(2):
        halo2.wait_recv((0, 1) if x == 0 else (-1,))
        for y in range(4):
            grad = input_rows(a2[...], d2, x, y)
            d1[x + 1, y + 1] = jnp.where(h3[x, y, 64:128].astype(F32) > 0, grad, 0.0).astype(BF16)
        halo1.start((-1,) if x == 0 else (0, 1))

    loads["w1"].wait()
    conv_matrix(w1_ref, rows, a1)
    total2[...] = filter_grad(d2, h3)
    away[0] = total2[rows_at((1 - core) * MIXED_ROWS, MIXED_ROWS)].astype(BF16)
    swaps = [remote(away.at[0], got0.at[0], core_send.at[0], core_recv.at[0], sibling)]
    swaps[0].start()
    haloc.wait_recv()
    swaps.append(remote(cb, cs, core_send.at[1], core_recv.at[1], sibling))
    swaps[1].start()

    def shift_coarse(cells_ref, to_ref):
        for nx, x in enumerate((1, 2 * core)):
            for y in range(4):
                cells = cells_ref[x, y]
                wide = cells.astype(F32)
                to_ref[0, nx, y] = moved(wide, -1).astype(BF16)
                to_ref[1, nx, y] = cells
                to_ref[2, nx, y] = moved(wide, 1).astype(BF16)

    shift_coarse(cb, c3)
    swaps[1].wait_recv()
    shift_coarse(cs, c3s)

    halo1.wait_recv()
    for x in (1 - core, core):
        for y in range(4):
            ub[x + 1, y + 1] = input_rows(a1[...], d1, x, y).astype(BF16)
        if len(swaps) == 2:
            swaps.append(remote(ub.at[x + 1, pl.ds(1, 4)], us, core_send.at[2], core_recv.at[2], sibling))
            swaps[2].start()
    total1[...] = filter_grad(d1, up3)
    away[1] = total1[rows_at((1 - core) * MIXED_ROWS, MIXED_ROWS)].astype(BF16)
    swaps.append(remote(away.at[1], got0.at[1], core_send.at[3], core_recv.at[3], sibling))
    swaps[3].start()

    def ring_start(part):
        axis = ORDERS[part][0]
        copies = []
        for chunk in range(CHUNKS):
            for j in RING:
                to = (place[axis] + j) % 4
                copies.append(remote(
                    held.at[rows_at(part * PART + to * QUARTER + chunk * CHUNK, CHUNK)],
                    got1.at[part, j - 1, pl.ds(chunk * CHUNK, CHUNK)],
                    ring_send.at[0, part, j - 1, chunk], ring_recv.at[0, part, j - 1, chunk], device(**{axis: to})))
                copies[-1].start()
        return copies

    swaps[2].wait_recv()
    fine = (lambda row: ub[1 + core, 1 + row], lambda row: us[row])
    rings = []
    for nx in range(2):
        for py in range(2):
            for pz in range(2):
                result = class_grad(fine, (c3, c3s), nx, py, pz).astype(BF16)
                n = 0
                for ky, _ in tap_choices(py):
                    for kz, _ in tap_choices(pz):
                        to = nx * PART + (4 * ky + kz) * 64
                        held[to : to + 64] = result[:, n * 128 : n * 128 + 128]
                        n += 1
        rings.append(ring_start(nx))
    swaps[0].wait_recv()
    swaps[3].wait_recv()
    mine = rows_at(core * MIXED_ROWS, MIXED_ROWS)
    sum2 = total2[mine] + got0[0].astype(F32)
    sum1 = total1[mine] + got0[1].astype(F32)
    for at, rows_of in enumerate((sum2[:, :128], sum1[:, :128], sum2[:, 128:] + sum1[:, 128:])):
        to = 2 * PART + at * MIXED_ROWS
        held[to : to + MIXED_ROWS] = rows_of.astype(BF16)
    held[2 * PART + 3 * MIXED_ROWS :] = jnp.zeros((PART - 3 * MIXED_ROWS, 128), BF16)
    rings.append(ring_start(2))

    home = [place[ORDERS[part][0]] for part in range(3)]
    seat = [place[ORDERS[part][1]] * 4 + place[ORDERS[part][2]] for part in range(3)]
    start = [core * HALF + part * PART + home[part] * QUARTER for part in range(3)]
    planes = [None] * 3
    for part in (0, 1, 2):
        for copy in rings[part]:
            copy.wait_recv()
        total = held[rows_at(part * PART + home[part] * QUARTER, QUARTER)].astype(F32)
        for j in range(3):
            total = total + got1[part, j].astype(F32)
        own1[part] = total.astype(BF16)
        planes[part] = []
        for j, step in enumerate(PLANE):
            there = plane_place(part, step)
            planes[part].append(remote(own1.at[part, rows_at((there[0] * 4 + there[1]) * PIECE, PIECE)],
                                       got2.at[part, j], plane_send.at[0, part, j], plane_recv.at[0, part, j],
                                       plane_peer(part, step)))
            planes[part][-1].start()
    sent = rings[0] + rings[1] + rings[2] + planes[0] + planes[1] + planes[2] + swaps

    spread = [None] * 3
    for part in (0, 1, 2):
        for copy in planes[part]:
            copy.wait_recv()
        total = own1[part, rows_at(seat[part] * PIECE, PIECE)].astype(F32)
        for j in range(15):
            total = total + got2[part, j].astype(F32)
        block = out_ref.at[rows_at(start[part] + seat[part] * PIECE, PIECE)]
        out_ref[rows_at(start[part] + seat[part] * PIECE, PIECE)] = total.astype(BF16)
        spread[part] = []
        for j, step in enumerate(PLANE):
            spread[part].append(remote(block, block, plane_send.at[1, part, j], plane_recv.at[1, part, j],
                                       plane_peer(part, step)))
            spread[part][-1].start()
    halou.start()
    shares, writes = [], []

    def write(from_row):
        block = rows_at(from_row, QUARTER)
        writes.append(pltpu.make_async_copy(out_ref.at[block], out_any.at[block], written.at[len(writes)]))
        writes[-1].start()

    def share(from_row):
        block = out_ref.at[rows_at(from_row, QUARTER)]
        at = 4 + len(shares)
        shares.append(remote(block, block, core_send.at[at], core_recv.at[at], sibling))
        shares[-1].start()
        write(from_row)

    back = [None] * 3
    for part in range(3):
        axis = ORDERS[part][0]
        for copy in spread[part]:
            copy.wait_recv()
        back[part] = {j: [] for j in RING}
        for chunk in range(CHUNKS):
            block = out_ref.at[rows_at(start[part] + chunk * CHUNK, CHUNK)]
            for j in RING:
                copy = remote(block, block, ring_send.at[1, part, j - 1, chunk], ring_recv.at[1, part, j - 1, chunk],
                              device(**{axis: (place[axis] + j) % 4}))
                copy.start()
                back[part][j].append(copy)
                sent.append(copy)
        share(start[part])
    halou.wait_recv()
    input_grad(ub, wt_ref, loads["wt"], ig_ref)
    for j in (1, 3, 2):
        for part in range(3):
            for copy in back[part][j]:
                copy.wait_recv()
            share(core * HALF + part * PART + (home[part] + 4 - j) % 4 * QUARTER)
    away_rows = (1 - core) * HALF
    order = [(0, part) for part in range(3)] + [(j, part) for j in (1, 3, 2) for part in range(3)]
    for copy, (j, part) in zip(shares, order):
        copy.wait_recv()
        write(away_rows + part * PART + (home[part] + 4 - j) % 4 * QUARTER)
    sent += spread[0] + spread[1] + spread[2] + shares
    for copy in sent:
        copy.wait_send()
    for halo in (halo1, halou, haloc):
        halo.wait_send()
    for copy in writes:
        copy.wait()


def input_grad(ub, wt_ref, load, ig_ref):
    load.wait()
    sums = []
    for half in range(2):
        around = jnp.concatenate(
            [ub[:, 2 * row : 2 * row + 4, :, half * 128 : half * 128 + 128].reshape(1024, 128) for row in range(2)],
            axis=1)
        filters = jnp.concatenate(
            [jnp.concatenate([wt_ref[4 * at + kz] for at in range(16)], axis=0) for kz in (1 - half, 3 - half)], axis=1)
        sums.append(lax.dot_general(filters, around, (((0,), (0,)), ((), ())), preferred_element_type=F32))
    even, odd = sums
    for row in range(2):
        lanes = slice(row * 128, row * 128 + 128)
        ig_ref[row] = (even[:128, lanes] + moved(even[128:, lanes], 1)
                       + odd[128:, lanes] + moved(odd[:128, lanes], -1)).astype(BF16)


def widen(scale, rows_any, ig_rows_any, ig_any, tconv_any, one_any, two_any,
          rows_ref, ig_rows_ref, ig_ref, tconv_ref, one_ref, two_ref, load, done):
    spans = [half * HALF + part * PART for part in (2, 0, 1) for half in range(2)]
    reads = [pltpu.make_async_copy(rows_any.at[pl.ds(start, PART)], rows_ref.at[pl.ds(start, PART)], load.at[at])
             for at, start in enumerate(spans)]
    reads.append(pltpu.make_async_copy(ig_rows_any, ig_rows_ref, load.at[len(spans)]))
    for copy in reads:
        copy.start()
    writes = []

    def write(source, to):
        writes.append(pltpu.make_async_copy(source, to, done.at[len(writes)]))
        writes[-1].start()

    for copy in reads[:2]:
        copy.wait()

    def piece(kind, start, size):
        half, inside = start // MIXED_ROWS, start % MIXED_ROWS
        at = half * HALF + 2 * PART + kind * MIXED_ROWS + inside
        many = min(size, MIXED_ROWS - inside)
        found = rows_ref[at : at + many].astype(F32) * scale
        return found if many == size else jnp.concatenate([found, piece(kind, start + many, size - many)], axis=0)

    for a in range(3):
        for b in range(3):
            low2, low1, high = (piece(kind, ((2 - a) * 3 + 2 - b) * 64, 64) for kind in range(3))
            tap = 9 * a + 3 * b
            two_ref[tap] = low2[:, :64]
            two_ref[tap + 1] = low2[:, 64:]
            two_ref[tap + 2] = high[:, :64]
            one_ref[tap] = low1[:, :64]
            one_ref[tap + 1] = low1[:, 64:]
            one_ref[tap + 2] = high[:, 64:]
        write(two_ref.at[pl.ds(9 * a, 9)], two_any.at[pl.ds(9 * a, 9)])
        write(one_ref.at[pl.ds(9 * a, 9)], one_any.at[pl.ds(9 * a, 9)])
    for at, kx in enumerate((1, 2, 3, 0), 2):
        reads[at].wait()
        cells = rows_ref[spans[at] : spans[at] + PART].astype(F32) * scale
        tconv_ref[16 * kx : 16 * kx + 16] = cells.reshape(16, 64, 128)
        write(tconv_ref.at[pl.ds(16 * kx, 16)], tconv_any.at[pl.ds(16 * kx, 16)])
    reads[6].wait()
    ig_ref[:, 0] = jnp.swapaxes(ig_rows_ref[...], 0, 1)
    write(ig_ref, ig_any)
    for copy in writes:
        copy.wait()


def shards(counts, coarse_input, upsampled, hidden_one, hidden_two, cotangent,
           tconv_weight, conv_one_weight, conv_two_weight):
    channels, planes, across, length = cotangent.shape
    scale = 1.0 / math.sqrt(planes * counts[0] * across * counts[1] * length)
    vmem, anywhere = pl.BlockSpec(memory_space=pltpu.VMEM), pl.BlockSpec(memory_space=pl.ANY)
    args = (coarse_input, upsampled, hidden_one, hidden_two, cotangent, tconv_weight, conv_one_weight, conv_two_weight)
    haloed = pltpu.VMEM((4, 6, channels, length), BF16)
    shifted = pltpu.VMEM((2, 4, 256, length), BF16)
    dma = pltpu.SemaphoreType.DMA
    input_rows, total = pl.pallas_call(
        functools.partial(section, counts),
        out_shape=(jax.ShapeDtypeStruct((2, 128, 128), BF16), jax.ShapeDtypeStruct((ROWS, 128), BF16)),
        in_specs=[pl.BlockSpec(memory_space=pltpu.HBM)] * 8,
        out_specs=(vmem, anywhere),
        scratch_shapes=[pltpu.VMEM(arg.shape, arg.dtype) for arg in args] + [
            haloed, haloed, haloed, pltpu.VMEM((3, 4, 128, 128), BF16),
            pltpu.VMEM((4, channels, length), BF16), pltpu.VMEM((3, 4, 128, 128), BF16),
            shifted, shifted, pltpu.VMEM((3, 2, 4, 128, 128), BF16), pltpu.VMEM((3, 2, 4, 128, 128), BF16),
            pltpu.VMEM((CONV_ROWS, 256), BF16), pltpu.VMEM((192, CONV_ROWS), BF16), pltpu.VMEM((192, CONV_ROWS), BF16),
            pltpu.VMEM((length, length), BF16), pltpu.VMEM((CONV_ROWS, 256), F32), pltpu.VMEM((CONV_ROWS, 256), F32),
            pltpu.VMEM((2, MIXED_ROWS, 256), BF16), pltpu.VMEM((2, MIXED_ROWS, 256), BF16),
            pltpu.VMEM((HALF, 128), BF16),
            pltpu.VMEM((3, 3, QUARTER, 128), BF16),
            pltpu.VMEM((3, 15, PIECE, 128), BF16),
            pltpu.VMEM((3, QUARTER, 128), BF16),
            pltpu.VMEM((ROWS, 128), BF16),
            dma((8,)), dma((4, 8)), dma((4, 8)), dma((16,)), dma((16,)),
            dma((2, 3, 3, CHUNKS)), dma((2, 3, 3, CHUNKS)), dma((2, 3, 15)), dma((2, 3, 15)), dma((24,)),
        ],
        compiler_params=pltpu.CompilerParams(collective_id=0, has_side_effects=True, vmem_limit_bytes=VMEM_BYTES),
    )(*args)

    shapes = (((128, 1, 2, 128), BF16), ((64, 64, 128), F32), ((27, 64, 64), F32), ((27, 64, 64), F32))
    return pl.pallas_call(
        functools.partial(widen, scale),
        out_shape=tuple(jax.ShapeDtypeStruct(*shape) for shape in shapes),
        in_specs=[anywhere, anywhere],
        out_specs=(anywhere,) * 4,
        scratch_shapes=[pltpu.VMEM((ROWS, 128), BF16), pltpu.VMEM((2, 128, 128), BF16)]
        + [pltpu.VMEM(*shape) for shape in shapes] + [dma((7,)), dma((11,))],
        compiler_params=pltpu.CompilerParams(vmem_limit_bytes=VMEM_BYTES),
    )(total, input_rows)


def solution(mesh):
    cells = P(None, "gx", "gy", None)
    return jax.shard_map(
        functools.partial(shards, (mesh.shape["gx"], mesh.shape["gy"])),
        mesh=mesh,
        in_specs=(cells,) * 5 + (P(),) * 3,
        out_specs=(cells, P(), P(), P()),
        check_vma=False,
    )
```
